128 devices in a mesh: dp: 16 (over x_hi, y, core), tensor: 8 (over x_lo, z).
Axes of the slice: x: 4 (x_hi: 2, x_lo: 2; x = x_hi * 2 + x_lo), y: 4, z: 4, core: 2. Of those that a mesh axis runs over, the one named last changes fastest.
Arguments:
- inputs: bfloat16 [32, 1024, 1024], P('dp', 'tensor'), may hold values from -6 to 6
- segments: int32 [32, 1024], P('dp'), may hold values from 0 to 2, as said below
- cotangent: bfloat16 [32, 1024, 1024], P('dp', 'tensor'), may hold values from -6 to 6
- query_weight: float32 [1024, 2048], P('dp', 'tensor'), may hold values from -0.1875 to 0.1875
- query_first: float32 [1024, 2048], P('dp', 'tensor'), may hold values from -112 to 112
- query_second: float32 [1024, 2048], P('dp', 'tensor'), may hold values from 1409.024 to 5570.56
- key_projection_weight: float32 [1024, 1024], P('dp', 'tensor'), may hold values from -0.1875 to 0.1875
- key_first_moment: float32 [1024, 1024], P('dp', 'tensor'), may hold values from -128 to 128
- key_second_moment: float32 [1024, 1024], P('dp', 'tensor'), may hold values from 2490.368 to 9830.4
- value_projection_weight: float32 [1024, 1024], P('dp', 'tensor'), may hold values from -0.1875 to 0.1875
- value_first_moment: float32 [1024, 1024], P('dp', 'tensor'), may hold values from -112 to 112
- value_second_moment: float32 [1024, 1024], P('dp', 'tensor'), may hold values from 1409.024 to 5570.56
- out_weight: float32 [2048, 1024], P('tensor', 'dp'), may hold values from -1 to 1
- out_first: float32 [2048, 1024], P('tensor', 'dp'), may hold values from -20 to 20
- out_second: float32 [2048, 1024], P('tensor', 'dp'), may hold values from 56.96 to 227.2
- gate_weight: float32 [1024, 3072], P('dp', 'tensor'), may hold values from -0.1875 to 0.1875
- gate_first: float32 [1024, 3072], P('dp', 'tensor'), may hold values from -40 to 40
- gate_second: float32 [1024, 3072], P('dp', 'tensor'), may hold values from 202.06934 to 808.27734
- up_weight: float32 [1024, 3072], P('dp', 'tensor'), may hold values from -0.1875 to 0.1875
- up_first: float32 [1024, 3072], P('dp', 'tensor'), may hold values from -40 to 40
- up_second: float32 [1024, 3072], P('dp', 'tensor'), may hold values from 202.06934 to 808.27734
- down_weight: float32 [3072, 1024], P('tensor', 'dp'), may hold values from -0.109375 to 0.109375
- down_first: float32 [3072, 1024], P('tensor', 'dp'), may hold values from -64 to 64
- down_second: float32 [3072, 1024], P('tensor', 'dp'), may hold values from 622.592 to 2490.368
- gains: float32 [2304], P('dp'), may hold values from 0.5 to 1.5
- gain_first: float32 [2304], P('dp'), may hold values from -125.989458 to 125.989458
- gain_second: float32 [2304], P('dp'), may hold values from 1111.4906 to 84473.28
Outputs:
- mixed_out: bfloat16 [32, 1024, 1024], P('dp', 'tensor')
- input_grad: float32 [32, 1024, 1024], P('dp', 'tensor')
- query_new: float32 [1024, 2048], P('dp', 'tensor')
- query_first_new: float32 [1024, 2048], P('dp', 'tensor')
- query_second_new: float32 [1024, 2048], P('dp', 'tensor')
- key_new: float32 [1024, 1024], P('dp', 'tensor')
- key_first_new: float32 [1024, 1024], P('dp', 'tensor')
- key_second_new: float32 [1024, 1024], P('dp', 'tensor')
- value_new: float32 [1024, 1024], P('dp', 'tensor')
- value_first_new: float32 [1024, 1024], P('dp', 'tensor')
- value_second_new: float32 [1024, 1024], P('dp', 'tensor')
- out_new: float32 [2048, 1024], P('tensor', 'dp')
- out_first_new: float32 [2048, 1024], P('tensor', 'dp')
- out_second_new: float32 [2048, 1024], P('tensor', 'dp')
- gate_new: float32 [1024, 3072], P('dp', 'tensor')
- gate_first_new: float32 [1024, 3072], P('dp', 'tensor')
- gate_second_new: float32 [1024, 3072], P('dp', 'tensor')
- up_new: float32 [1024, 3072], P('dp', 'tensor')
- up_first_new: float32 [1024, 3072], P('dp', 'tensor')
- up_second_new: float32 [1024, 3072], P('dp', 'tensor')
- down_new: float32 [3072, 1024], P('tensor', 'dp')
- down_first_new: float32 [3072, 1024], P('tensor', 'dp')
- down_second_new: float32 [3072, 1024], P('tensor', 'dp')
- gains_new: float32 [2304], P('dp')
- gain_first_new: float32 [2304], P('dp')
- gain_second_new: float32 [2304], P('dp')
The draws below stay inside these ranges and needn't reach their ends.
Inputs may be any that keep to these rules, and one draw needn't show every extreme that they name: `segments`: segment numbers start at 0 in every sequence and never fall; each sequence holds two or three documents of 64 positions or more; in each aligned block of 2 sequences one holds a document that begins before position 128 and runs to the end.
All inputs are finite; a program needn't handle non-finite values.
Results may differ from the reference program's by a relative error of at most 0.025.
Values may be sent and summed in bfloat16 or wider, within the bound.
No kernel may reach another device: no remote copies, remote signals or barrier semaphores. Data moves between devices by JAX's collectives and lax.ppermute only.
A program may use at most 192 MiB of HBM per device.

```python
import math
import jax
import jax.numpy as jnp
from jax import lax

MODEL_WIDTH = 1024
QUERY_HEADS = 16
KEY_VALUE_HEADS = 8
HEAD_SIZE = 128
FF = 3072
SEQS = 2
SEQUENCE_LENGTH = 1024
STEP = 10
BLK = 512
SEQ_ALL = 32
TOKEN_TOTAL = 32768
GAINS = 2304
WO_FAN = 40
N_TENSOR = 8


def draw_segments(key, part):
    key = jax.random.fold_in(key, 5)
    first_key, second_key, long_key, pick_key = jax.random.split(key, 4)
    first_cut = jax.random.randint(first_key, (SEQ_ALL, 1), SEQUENCE_LENGTH // 5, 2 * SEQUENCE_LENGTH // 5)
    second_cut = jax.random.randint(second_key, (SEQ_ALL, 1), 3 * SEQUENCE_LENGTH // 5, 4 * SEQUENCE_LENGTH // 5)
    long_cut = jax.random.randint(long_key, (SEQ_ALL, 1), SEQUENCE_LENGTH // 16, SEQUENCE_LENGTH // 8)
    chosen = jax.random.randint(pick_key, (SEQ_ALL // SEQS, 1), 0, SEQS)
    member = (jnp.arange(SEQ_ALL, dtype=jnp.int32) % SEQS).reshape(SEQ_ALL, 1)
    is_long = member == jnp.repeat(chosen, SEQS, axis=0)
    place = jnp.arange(SEQUENCE_LENGTH, dtype=jnp.int32)[None, :]
    drawn = (place >= first_cut).astype(jnp.int32) + (place >= second_cut).astype(jnp.int32)
    longer = (place >= long_cut).astype(jnp.int32)
    return jnp.where(is_long, longer, drawn).astype(jnp.int32)


def gain_levels():
    gain_level_values = jnp.concatenate([jnp.full((MODEL_WIDTH,), 2.0, jnp.float32), jnp.full((MODEL_WIDTH,), 0.8, jnp.float32), jnp.full((HEAD_SIZE,), 0.87 * QUERY_HEADS ** 0.5, jnp.float32), jnp.full((HEAD_SIZE,), 1.2 * KEY_VALUE_HEADS ** 0.5, jnp.float32)])
    return gain_level_values * TOKEN_TOTAL ** 0.5


def draw_gain_first(key, part):
    key = jax.random.fold_in(key, 11)
    spread = jax.random.uniform(key, (GAINS,), jnp.float32, -0.2, 0.2)
    return (spread * gain_levels()).astype(jnp.float32)


def draw_gain_second(key, part):
    key = jax.random.fold_in(key, 12)
    spread = jax.random.uniform(key, (GAINS,), jnp.float32, 0.0, math.log(4.0))
    gain_level_values = gain_levels()
    return (0.053 * gain_level_values * gain_level_values * jnp.exp(spread)).astype(jnp.float32)


def levels(stream_key, shape, shards, smallest, high):
    def one(dim, shards_of):
        steps = jax.random.uniform(jax.random.fold_in(jax.random.fold_in(stream_key, 6), dim), (shards_of,), jnp.float32, smallest / len(shards), high / len(shards))
        return jnp.repeat(jnp.exp(steps), shape[dim] // shards_of).reshape((-1,) + (1,) * (len(shape) - dim - 1))

    loudness = one(*shards[0])
    for cut in shards[1:]:
        loudness = loudness * one(*cut)
    return loudness


def bell_draw(key, dims, scale, most, cuts=(), held_as=jnp.bfloat16):
    gain = levels(key, dims, cuts, -0.22, 0.18) if cuts else 1.0
    values = jax.random.normal(key, dims, jnp.float32) * scale * gain
    return jnp.minimum(jnp.maximum(values, -most), most).astype(held_as)


def setup_inputs(seed: int = 0) -> dict:
    streams_of = jax.random.split(jax.random.key(seed), 28)
    return {
        "inputs": bell_draw(streams_of[0], (SEQ_ALL, SEQUENCE_LENGTH, MODEL_WIDTH), 1.0, 6.0, ((0, 16), (1, 8))),
        "segments": draw_segments(jax.random.fold_in(streams_of[27], 71), 0),
        "cotangent": bell_draw(streams_of[2], (SEQ_ALL, SEQUENCE_LENGTH, MODEL_WIDTH), 1.0, 6.0, ((0, 16), (1, 8))),
        "query_weight": bell_draw(streams_of[3], (MODEL_WIDTH, QUERY_HEADS * HEAD_SIZE), MODEL_WIDTH ** -0.5, 0.1875, ((0, 16), (1, 8)), jnp.float32),
        "query_first": bell_draw(streams_of[4], (MODEL_WIDTH, QUERY_HEADS * HEAD_SIZE), (0.1 * TOKEN_TOTAL ** 0.5), 112.0, ((0, 16), (1, 8)), jnp.float32),
        "query_second": jnp.clip(jnp.exp(math.log(5570.56) - 1.3745983 * jax.random.uniform(streams_of[5], (MODEL_WIDTH, QUERY_HEADS * HEAD_SIZE), jnp.float32) ** levels(streams_of[5], (MODEL_WIDTH, QUERY_HEADS * HEAD_SIZE), ((0, 16), (1, 8)), -0.2, 0.2)), 1409.024, 5570.56),
        "key_projection_weight": bell_draw(streams_of[6], (MODEL_WIDTH, KEY_VALUE_HEADS * HEAD_SIZE), MODEL_WIDTH ** -0.5, 0.1875, ((0, 16), (1, 8)), jnp.float32),
        "key_first_moment": bell_draw(streams_of[7], (MODEL_WIDTH, KEY_VALUE_HEADS * HEAD_SIZE), (0.133 * TOKEN_TOTAL ** 0.5), 128.0, ((0, 16), (1, 8)), jnp.float32),
        "key_second_moment": jnp.clip(jnp.exp(math.log(9830.4) - 1.3730492 * jax.random.uniform(streams_of[8], (MODEL_WIDTH, KEY_VALUE_HEADS * HEAD_SIZE), jnp.float32) ** levels(streams_of[8], (MODEL_WIDTH, KEY_VALUE_HEADS * HEAD_SIZE), ((0, 16), (1, 8)), -0.2, 0.2)), 2490.368, 9830.4),
        "value_projection_weight": bell_draw(streams_of[9], (MODEL_WIDTH, KEY_VALUE_HEADS * HEAD_SIZE), MODEL_WIDTH ** -0.5, 0.1875, ((0, 16), (1, 8)), jnp.float32),
        "value_first_moment": bell_draw(streams_of[10], (MODEL_WIDTH, KEY_VALUE_HEADS * HEAD_SIZE), (0.1 * TOKEN_TOTAL ** 0.5), 112.0, ((0, 16), (1, 8)), jnp.float32),
        "value_second_moment": jnp.clip(jnp.exp(math.log(5570.56) - 1.3745983 * jax.random.uniform(streams_of[11], (MODEL_WIDTH, KEY_VALUE_HEADS * HEAD_SIZE), jnp.float32) ** levels(streams_of[11], (MODEL_WIDTH, KEY_VALUE_HEADS * HEAD_SIZE), ((0, 16), (1, 8)), -0.2, 0.2)), 1409.024, 5570.56),
        "out_weight": bell_draw(streams_of[12], (QUERY_HEADS * HEAD_SIZE, MODEL_WIDTH), WO_FAN ** -0.5, 1.0, ((0, 8), (1, 16)), jnp.float32),
        "out_first": bell_draw(streams_of[13], (QUERY_HEADS * HEAD_SIZE, MODEL_WIDTH), (0.64 * (TOKEN_TOTAL * SEQUENCE_LENGTH ** -1) ** 0.5), 20.0, ((0, 8), (1, 16)), jnp.float32),
        "out_second": jnp.clip(jnp.exp(math.log(227.2) - 1.3834814 * jax.random.uniform(streams_of[14], (QUERY_HEADS * HEAD_SIZE, MODEL_WIDTH), jnp.float32) ** levels(streams_of[14], (QUERY_HEADS * HEAD_SIZE, MODEL_WIDTH), ((0, 8), (1, 16)), -0.2, 0.2)), 56.96, 227.2),
        "gate_weight": bell_draw(streams_of[15], (MODEL_WIDTH, FF), MODEL_WIDTH ** -0.5, 0.1875, ((0, 16), (1, 8)), jnp.float32),
        "gate_first": bell_draw(streams_of[16], (MODEL_WIDTH, FF), (0.065 * (MODEL_WIDTH * TOKEN_TOTAL * FF ** -1) ** 0.5), 40.0, ((0, 16), (1, 8)), jnp.float32),
        "gate_second": jnp.clip(jnp.exp(math.log(808.27734) - 1.3862944 * jax.random.uniform(streams_of[17], (MODEL_WIDTH, FF), jnp.float32) ** levels(streams_of[17], (MODEL_WIDTH, FF), ((0, 16), (1, 8)), -0.2, 0.2)), 202.06934, 808.27734),
        "up_weight": bell_draw(streams_of[18], (MODEL_WIDTH, FF), MODEL_WIDTH ** -0.5, 0.1875, ((0, 16), (1, 8)), jnp.float32),
        "up_first": bell_draw(streams_of[19], (MODEL_WIDTH, FF), (0.065 * (MODEL_WIDTH * TOKEN_TOTAL * FF ** -1) ** 0.5), 40.0, ((0, 16), (1, 8)), jnp.float32),
        "up_second": jnp.clip(jnp.exp(math.log(808.27734) - 1.3862944 * jax.random.uniform(streams_of[20], (MODEL_WIDTH, FF), jnp.float32) ** levels(streams_of[20], (MODEL_WIDTH, FF), ((0, 16), (1, 8)), -0.2, 0.2)), 202.06934, 808.27734),
        "down_weight": bell_draw(streams_of[21], (FF, MODEL_WIDTH), FF ** -0.5, 0.109375, ((0, 8), (1, 16)), jnp.float32),
        "down_first": bell_draw(streams_of[22], (FF, MODEL_WIDTH), (0.067 * TOKEN_TOTAL ** 0.5), 64.0, ((0, 8), (1, 16)), jnp.float32),
        "down_second": jnp.clip(jnp.exp(math.log(2490.368) - 1.3862944 * jax.random.uniform(streams_of[23], (FF, MODEL_WIDTH), jnp.float32) ** levels(streams_of[23], (FF, MODEL_WIDTH), ((0, 8), (1, 16)), -0.2, 0.2)), 622.592, 2490.368),
        "gains": jnp.clip(1.0 + 0.1 * jax.random.normal(streams_of[24], (GAINS,), jnp.float32), 0.5, 1.5),
        "gain_first": draw_gain_first(jax.random.fold_in(streams_of[27], 71), 0),
        "gain_second": draw_gain_second(jax.random.fold_in(streams_of[27], 71), 0),
    }


@jax.custom_vjp
def lower_bound(v):
    return lax.optimization_barrier(v.astype(jnp.bfloat16)).astype(jnp.float32)

@jax.custom_vjp
def lower_backward(v):
    return v

def low_keep(v):
    return (lower_bound(v), None)

def low_pass(kept, grad):
    return (grad,)

def back_keep(v):
    return (v, None)

def back_low(kept, grad):
    return (lower_bound(grad),)
lower_bound.defvjp(low_keep, low_pass)
lower_backward.defvjp(back_keep, back_low)
norm_eps = 1e-06
rope_base = 1000000.0
beta_one = 0.9
beta_two = 0.95
adam_eps = 1e-08
decay_rate = 0.1
matrix_rate = 2.5
gain_rate = 0.5
doc_limit = 3
masked_value = -1000000000.0

def matrix_multiply(left, right):
    return jnp.dot(left, right, precision=lax.Precision.HIGHEST, preferred_element_type=jnp.float32)

def grouped_matmul(left, right, groups):
    cut = left.shape[-1] // groups
    total = jnp.zeros((left.shape[0], right.shape[1]), jnp.float32)
    for index in range(groups):
        total = total + lower_bound(matrix_multiply(left[:, index * cut:(index + 1) * cut], right[index * cut:(index + 1) * cut]))
    return total

def rms_scale(value_heads_rows):
    return value_heads_rows * lax.rsqrt(lax.optimization_barrier(jnp.mean(value_heads_rows * value_heads_rows, axis=-1, keepdims=True)) + norm_eps)

def rotate(value_heads_rows, cosine, sine):
    half = value_heads_rows.shape[-1] // 2
    turned = jnp.concatenate([-value_heads_rows[..., half:], value_heads_rows[..., :half]], axis=-1)
    return value_heads_rows * cosine + turned * sine

def positions(document_segment):
    before = jnp.zeros(document_segment.shape, jnp.int32)
    for level in range(doc_limit):
        count = lax.optimization_barrier(jnp.sum((document_segment == level).astype(jnp.int32), axis=-1, keepdims=True))
        before = before + jnp.where(document_segment > level, count, 0)
    return lax.broadcasted_iota(jnp.int32, document_segment.shape, document_segment.ndim - 1) - before

def rope_tables(document_segment, width):
    place = positions(document_segment).astype(jnp.float32)
    index = jnp.arange(width // 2, dtype=jnp.float32)
    inverse = jnp.exp(index * (-2.0 * math.log(rope_base) / width))
    angle = place[..., None] * inverse
    cosine = jnp.cos(angle)
    sine = jnp.sin(angle)
    return (jnp.concatenate([cosine, cosine], axis=-1), jnp.concatenate([sine, sine], axis=-1))

def attend_heads(query_heads_rows, key, value_heads_rows, document_segment):
    scale = HEAD_SIZE ** (-0.5)
    column_index = jnp.arange(SEQUENCE_LENGTH, dtype=jnp.int32)

    def block_rows(start):
        rows = lax.dynamic_slice_in_dim(query_heads_rows, start, BLK, 0)
        row_index = start + jnp.arange(BLK, dtype=jnp.int32)
        row_segment = lax.dynamic_slice_in_dim(document_segment, start, BLK, 0)
        scores = jnp.einsum('qgrd,kgd->grqk', rows, key, precision=lax.Precision.HIGHEST) * scale
        scores = lower_backward(scores)
        allowed = (row_segment[:, None] == document_segment[None, :]) & (column_index[None, :] <= row_index[:, None])
        scores = jnp.where(allowed, scores, masked_value)
        top = lax.optimization_barrier(jnp.max(scores, axis=-1, keepdims=True))
        raised = jnp.exp(scores - top)
        softened = lower_bound(raised / lax.optimization_barrier(jnp.sum(raised, axis=-1, keepdims=True)))
        return jnp.einsum('grqk,kgd->qgrd', softened, value_heads_rows, precision=lax.Precision.HIGHEST)
    starts = jnp.arange(SEQUENCE_LENGTH // BLK, dtype=jnp.int32) * BLK
    mixed_heads = lax.map(jax.checkpoint(block_rows), starts)
    return mixed_heads.reshape(SEQUENCE_LENGTH, QUERY_HEADS * HEAD_SIZE)

def layer(params, inputs, document_segment):
    query_mat, key_matrix, value_matrix, out_mat, gate_mat, up_mat, down_mat, gain_all = [lower_bound(param) for param in params]
    attn_gain = gain_all[:MODEL_WIDTH]
    feed_gain = gain_all[MODEL_WIDTH:2 * MODEL_WIDTH]
    query_gain = gain_all[2 * MODEL_WIDTH:2 * MODEL_WIDTH + HEAD_SIZE]
    key_gain = gain_all[2 * MODEL_WIDTH + HEAD_SIZE:]
    cosine, sine = rope_tables(document_segment, HEAD_SIZE)
    cosine = cosine[:, None, :]
    sine = sine[:, None, :]
    normalized_rows = lower_bound(rms_scale(inputs) * attn_gain)
    query_heads_rows = lower_backward(matrix_multiply(normalized_rows, query_mat)).reshape(SEQUENCE_LENGTH, QUERY_HEADS, HEAD_SIZE)
    key = lower_backward(matrix_multiply(normalized_rows, key_matrix)).reshape(SEQUENCE_LENGTH, KEY_VALUE_HEADS, HEAD_SIZE)
    value_heads_rows = lower_backward(lower_bound(matrix_multiply(normalized_rows, value_matrix))).reshape(SEQUENCE_LENGTH, KEY_VALUE_HEADS, HEAD_SIZE)
    query_heads_rows = lower_bound(rotate(rms_scale(query_heads_rows) * query_gain, cosine, sine))
    key = lower_bound(rotate(rms_scale(key) * key_gain, cosine, sine))
    mixed_heads = attend_heads(query_heads_rows.reshape(SEQUENCE_LENGTH, KEY_VALUE_HEADS, QUERY_HEADS // KEY_VALUE_HEADS, HEAD_SIZE), key, value_heads_rows, document_segment)
    mixed_heads = lower_backward(lower_bound(mixed_heads))
    middle = inputs + lower_backward(grouped_matmul(mixed_heads, out_mat, N_TENSOR))
    normed_two = lower_bound(rms_scale(middle) * feed_gain)
    gate_activation = lower_backward(matrix_multiply(normed_two, gate_mat))
    upper_bound = lower_backward(matrix_multiply(normed_two, up_mat))
    hidden_state = lower_bound(jax.nn.silu(gate_activation) * upper_bound)
    return middle + lower_backward(grouped_matmul(hidden_state, down_mat, N_TENSOR))

def adamw(weight, first, second, grad, rate):
    first_new = beta_one * first + (1.0 - beta_one) * grad
    second_new = beta_two * second + (1.0 - beta_two) * grad * grad
    ratio = first_new / (1.0 - beta_one ** STEP) / (jnp.sqrt(second_new / (1.0 - beta_two ** STEP)) + adam_eps)
    return (weight - rate * (ratio + decay_rate * weight), first_new, second_new)

def reference(inputs, segments, cotangent, query_weight, query_first, query_second, key_projection_weight, key_first_moment, key_second_moment, value_projection_weight, value_first_moment, value_second_moment, out_weight, out_first, out_second, gate_weight, gate_first, gate_second, up_weight, up_first, up_second, down_weight, down_first, down_second, gains, gain_first, gain_second):
    params = (query_weight, key_projection_weight, value_projection_weight, out_weight, gate_weight, up_weight, down_weight, gains)

    def per_sequence(total, items):
        row_input, row_segment, row_cotangent = items

        def forward(param_set, values):
            return layer(param_set, values, row_segment)
        result, pull = jax.vjp(forward, params, row_input.astype(jnp.float32))
        param_grads, grad_in = pull(row_cotangent.astype(jnp.float32))
        total = jax.tree.map(lambda left, right: left + right, total, param_grads)
        return (total, (result.astype(jnp.bfloat16), grad_in))
    start = jax.tree.map(jnp.zeros_like, params)
    sums, (outputs, input_grads) = lax.scan(per_sequence, start, (inputs, segments, cotangent))
    query_sum, key_sum, value_sum, out_sum, gate_sum, up_sum, down_sum, gain_sum = sums
    wide_rate = matrix_rate * MODEL_WIDTH ** (-0.5)
    query_new, query_first_new, query_second_new = adamw(query_weight, query_first, query_second, query_sum, wide_rate)
    key_new, key_first_new, key_second_new = adamw(key_projection_weight, key_first_moment, key_second_moment, key_sum, wide_rate)
    value_new, value_first_new, value_second_new = adamw(value_projection_weight, value_first_moment, value_second_moment, value_sum, wide_rate)
    out_new, out_first_new, out_second_new = adamw(out_weight, out_first, out_second, out_sum, matrix_rate * WO_FAN ** (-0.5))
    gate_new, gate_first_new, gate_second_new = adamw(gate_weight, gate_first, gate_second, gate_sum, wide_rate)
    up_new, up_first_new, up_second_new = adamw(up_weight, up_first, up_second, up_sum, wide_rate)
    down_new, down_first_new, down_second_new = adamw(down_weight, down_first, down_second, down_sum, matrix_rate * FF ** (-0.5))
    gains_new, gain_first_new, gain_second_new = adamw(gains, gain_first, gain_second, gain_sum, gain_rate)
    return (outputs, input_grads, query_new, query_first_new, query_second_new, key_new, key_first_new, key_second_new, value_new, value_first_new, value_second_new, out_new, out_first_new, out_second_new, gate_new, gate_first_new, gate_second_new, up_new, up_first_new, up_second_new, down_new, down_first_new, down_second_new, gains_new, gain_first_new, gain_second_new)
```

```python
import math

import jax
import jax.numpy as jnp
from jax import lax
from jax.sharding import Mesh
from jax.sharding import PartitionSpec as P

MODEL_WIDTH = 1024
QUERY_HEADS = 16
KEY_VALUE_HEADS = 8
HEAD_SIZE = 128
FF = 3072
STEP = 10
WO_FAN = 40

norm_eps = 1e-06
rope_base = 1000000.0
beta_one = 0.9
beta_two = 0.95
adam_eps = 1e-08
decay_rate = 0.1
matrix_rate = 2.5
gain_rate = 0.5
doc_limit = 3
masked_value = -1000000000.0

bf = jnp.bfloat16
f32 = jnp.float32
X = ("xh", "xl")
ALL = ("xh", "y", "c", "xl", "z")
DP = ("xh", "y", "c")
TENSOR = ("xl", "z")


def rms_parts(rows):
    inverse = lax.rsqrt(jnp.mean(rows * rows, axis=-1, keepdims=True) + norm_eps)
    return (rows * inverse, inverse)


def norm_back(grad, scaled, inverse, gain):
    pushed = grad * gain
    return inverse * (pushed - scaled * jnp.mean(pushed * scaled, axis=-1, keepdims=True))


def rotate(rows, cosine, sine):
    half = rows.shape[-1] // 2
    turned = jnp.concatenate([-rows[..., half:], rows[..., :half]], axis=-1)
    return rows * cosine + turned * sine


def unrotate(grad, cosine, sine):
    half = grad.shape[-1] // 2
    moved = grad * sine
    turned = jnp.concatenate([moved[..., half:], -moved[..., :half]], axis=-1)
    return grad * cosine + turned


def positions(segment):
    before = jnp.zeros(segment.shape, jnp.int32)
    for level in range(doc_limit):
        count = jnp.sum((segment == level).astype(jnp.int32), axis=-1, keepdims=True)
        before = before + jnp.where(segment > level, count, 0)
    return lax.broadcasted_iota(jnp.int32, segment.shape, segment.ndim - 1) - before


def rope_tables(segment, width):
    place = positions(segment).astype(f32)
    index = jnp.arange(width // 2, dtype=f32)
    inverse = jnp.exp(index * (-2.0 * math.log(rope_base) / width))
    angle = place[..., None] * inverse
    cosine = jnp.cos(angle)
    sine = jnp.sin(angle)
    return (jnp.concatenate([cosine, cosine], axis=-1), jnp.concatenate([sine, sine], axis=-1))


def ring(count, step):
    return [(i, (i + step) % count) for i in range(count)]


def swap(value, axis):
    return lax.ppermute(value, axis, ring(2, 1))


def gather_ring(value, axis, place, dim):
    shape = value.shape[:dim] + (4,) + value.shape[dim:]
    whole = jnp.zeros(shape, value.dtype)
    whole = lax.dynamic_update_slice_in_dim(whole, jnp.expand_dims(value, dim), place, dim)
    for step in (1, 3, 2):
        other = lax.ppermute(value, axis, ring(4, step))
        whole = lax.dynamic_update_slice_in_dim(
            whole, jnp.expand_dims(other, dim), (place + 4 - step) % 4, dim
        )
    return whole


def scatter_sum(value, axis, place, dim):
    def part(at):
        return lax.dynamic_index_in_dim(value, at % 4, dim, keepdims=False)

    total = part(place).astype(f32)
    for step in (2, 1, 3):
        total = total + lax.ppermute(part(place + step), axis, ring(4, step)).astype(f32)
    return total


def by_sequence(value, xl):
    keep = lax.dynamic_index_in_dim(value, xl, 0, keepdims=False)
    other = swap(lax.dynamic_index_in_dim(value, 1 - xl, 0, keepdims=False), "xl")
    first = xl == 0
    return jnp.stack([jnp.where(first, keep, other), jnp.where(first, other, keep)])


def adamw(weight, first, second, grad, rate):
    first_new = beta_one * first + (1.0 - beta_one) * grad
    second_new = beta_two * second + (1.0 - beta_two) * grad * grad
    ratio = (
        first_new
        / (1.0 - beta_one**STEP)
        / (jnp.sqrt(second_new / (1.0 - beta_two**STEP)) + adam_eps)
    )
    return (weight - rate * (ratio + decay_rate * weight), first_new, second_new)


def dot(left, right, dims):
    return lax.dot_general(left, right, (dims, ((), ())), preferred_element_type=f32)


def gather_weight(shard, y, x, c):
    n = shard.shape[1]
    rows = gather_ring(shard, "y", y, 0)
    rows = gather_ring(rows, X, x, 0)
    other = swap(rows, "c")
    first = c == 0
    both = jnp.stack([jnp.where(first, rows, other), jnp.where(first, other, rows)])
    both = both.reshape(2, 2, 2, 4, 64, n)
    return both.transpose(1, 3, 0, 4, 2, 5).reshape(MODEL_WIDTH, 2, n)


def scatter_weight(grad, c):
    n = grad.shape[2]
    grad = grad.astype(bf).reshape(2, 4, 2, 64, 2, n).transpose(2, 0, 4, 1, 3, 5)
    grad = grad.reshape(2, 4, 4, 64, n)
    keep = lax.dynamic_index_in_dim(grad, c, 0, keepdims=False)
    other = swap(lax.dynamic_index_in_dim(grad, 1 - c, 0, keepdims=False), "c")
    mine = (keep.astype(f32) + other.astype(f32)).astype(bf)
    mine = lax.psum_scatter(mine, X, scatter_dimension=0, tiled=False)
    mine = lax.psum_scatter(mine, "y", scatter_dimension=0, tiled=False)
    return mine.astype(f32)


def per_device(
    inputs,
    segments,
    cotangent,
    query_weight,
    query_first,
    query_second,
    key_weight,
    key_first,
    key_second,
    value_weight,
    value_first,
    value_second,
    out_weight,
    out_first,
    out_second,
    gate_weight,
    gate_first,
    gate_second,
    up_weight,
    up_first,
    up_second,
    down_weight,
    down_first,
    down_second,
    gains,
    gain_first,
    gain_second,
):
    width = inputs.shape[2]
    length = segments.shape[1]
    block = 512
    scale = HEAD_SIZE ** (-0.5)
    xl, z, y, c = (lax.axis_index(name) for name in ("xl", "z", "y", "c"))
    x = lax.axis_index(X)

    attn_pack = jnp.concatenate([query_weight, key_weight, value_weight], axis=1).astype(bf)
    rest_pack = jnp.concatenate(
        [out_weight.T, gate_weight, up_weight, down_weight.T], axis=1
    ).astype(bf)
    gain_all = lax.all_to_all(
        jnp.broadcast_to(gains.astype(bf).astype(f32)[None], (16,) + gains.shape), DP, 0, 0, tiled=True
    ).reshape(-1)
    attn_gain = gain_all[:width]
    feed_gain = gain_all[width : 2 * width]
    query_gain = gain_all[2 * width : 2 * width + HEAD_SIZE]
    key_gain = gain_all[2 * width + HEAD_SIZE :]

    base = by_sequence(inputs, xl).astype(f32)
    push = by_sequence(cotangent, xl)
    segment = lax.dynamic_index_in_dim(segments, xl, 0, keepdims=False)
    cosine, sine = rope_tables(segment, HEAD_SIZE)
    cosine = cosine[:, None, :]
    sine = sine[:, None, :]

    normed_one, inverse_one = rms_parts(base)
    rows_one = gather_ring((normed_one * attn_gain).astype(bf), "z", z, 1).reshape(length, width)
    attn_all = gather_weight(attn_pack, y, x, c)
    rest_all = gather_weight(rest_pack, y, x, c)
    wq = attn_all[:, :, :256].reshape(width, 512)
    wk = attn_all[:, :, 256:384].reshape(width, 256)
    wv = attn_all[:, :, 384:].reshape(width, 256)
    wo = rest_all[:, :, :256].reshape(width, 512)
    wg = rest_all[:, :, 256:640].reshape(width, 768)
    wu = rest_all[:, :, 640:1024].reshape(width, 768)
    wd = rest_all[:, :, 1024:].reshape(width, 768)
    push_all = gather_ring(push, "z", z, 1).reshape(length, width)

    query = dot(rows_one, wq, ((1,), (0,)))
    key = dot(rows_one, wk, ((1,), (0,)))
    value = dot(rows_one, wv, ((1,), (0,))).astype(bf).reshape(length, 2, HEAD_SIZE)
    query_shaped, query_inverse = rms_parts(query.reshape(length, 4, HEAD_SIZE))
    key_shaped, key_inverse = rms_parts(key.reshape(length, 2, HEAD_SIZE))
    query_rot = (
        rotate(query_shaped * query_gain, cosine, sine).astype(bf).reshape(length, 2, 2, HEAD_SIZE)
    )
    key_rot = rotate(key_shaped * key_gain, cosine, sine).astype(bf)
    mixed_parts = []
    log_totals = []
    masks = []
    for first in range(0, length, block):
        stop = first + block
        row_index = first + jnp.arange(block, dtype=jnp.int32)
        column_index = jnp.arange(stop, dtype=jnp.int32)
        allowed = (segment[first:stop, None] == segment[None, :stop]) & (
            column_index[None, :] <= row_index[:, None]
        )
        masks.append(allowed)
        scores = (
            jnp.einsum(
                "qgrd,kgd->grqk",
                query_rot[first:stop],
                key_rot[:stop],
                preferred_element_type=f32,
            )
            * scale
        )
        scores = jnp.where(allowed, scores, masked_value)
        top = jnp.max(scores, axis=-1, keepdims=True)
        raised = jnp.exp(scores - top)
        total = jnp.sum(raised, axis=-1, keepdims=True)
        log_totals.append(top + jnp.log(total))
        softened = (raised / total).astype(bf)
        mixed_parts.append(
            jnp.einsum("grqk,kgd->qgrd", softened, value[:stop], preferred_element_type=f32)
        )
    mixed_heads = jnp.concatenate(mixed_parts, axis=0).reshape(length, 512).astype(bf)
    out_part = dot(mixed_heads, wo, ((1,), (1,))).astype(bf).reshape(2, 4, 128, width)
    middle = base + scatter_sum(out_part, "z", z, 1)
    normed_two, inverse_two = rms_parts(middle)
    rows_two = gather_ring((normed_two * feed_gain).astype(bf), "z", z, 1).reshape(length, width)
    gate = dot(rows_two, wg, ((1,), (0,)))
    up = dot(rows_two, wu, ((1,), (0,)))
    sigma = jax.nn.sigmoid(gate)
    swish = gate * sigma
    hidden = (swish * up).astype(bf)
    feed_part = dot(hidden, wd, ((1,), (1,))).astype(bf).reshape(2, 4, 128, width)
    result = (middle + scatter_sum(feed_part, "z", z, 1)).astype(bf)

    d_hidden = dot(push_all, wd, ((1,), (0,)))
    grad_down = dot(push_all, hidden, ((0,), (0,)))
    slope = sigma * (1.0 + gate * (1.0 - sigma))
    d_gate = (d_hidden * up * slope).astype(bf)
    d_up = (d_hidden * swish).astype(bf)
    grad_gate = dot(rows_two, d_gate, ((0,), (0,)))
    grad_up = dot(rows_two, d_up, ((0,), (0,)))
    second_part = dot(d_gate, wg, ((1,), (1,))) + dot(d_up, wu, ((1,), (1,)))
    two_share = scatter_sum(second_part.astype(bf).reshape(2, 4, 128, width), "z", z, 1)
    feed_gain_grad = jnp.sum(two_share * normed_two, axis=(0, 1))
    middle_grad = push.astype(f32) + norm_back(two_share, normed_two, inverse_two, feed_gain)
    mixed_rows = gather_ring(middle_grad.astype(bf), "z", z, 1).reshape(length, width)
    grad_out = dot(mixed_rows, mixed_heads, ((0,), (0,)))
    mixed_back = dot(mixed_rows, wo, ((1,), (0,))).astype(bf).reshape(length, 2, 2, HEAD_SIZE)
    query_back_parts = []
    key_back = jnp.zeros((length, 2, HEAD_SIZE), f32)
    value_back = jnp.zeros((length, 2, HEAD_SIZE), f32)
    for number, first in enumerate(range(0, length, block)):
        stop = first + block
        rows = query_rot[first:stop]
        keys = key_rot[:stop]
        scores = jnp.einsum("qgrd,kgd->grqk", rows, keys, preferred_element_type=f32) * scale
        scores = jnp.where(masks[number], scores, masked_value)
        softened = jnp.exp(scores - log_totals[number])
        grad_rows = mixed_back[first:stop]
        value_step = jnp.einsum(
            "grqk,qgrd->kgd", softened.astype(bf), grad_rows, preferred_element_type=f32
        )
        pushed = jnp.einsum("qgrd,kgd->grqk", grad_rows, value[:stop], preferred_element_type=f32)
        centre = jnp.sum(softened * pushed, axis=-1, keepdims=True)
        score_back = (softened * (pushed - centre)).astype(bf)
        query_back_parts.append(
            jnp.einsum("grqk,kgd->qgrd", score_back, keys, preferred_element_type=f32) * scale
        )
        key_step = (
            jnp.einsum("grqk,qgrd->kgd", score_back, rows, preferred_element_type=f32) * scale
        )
        padding = ((0, length - stop), (0, 0), (0, 0))
        key_back = key_back + jnp.pad(key_step, padding)
        value_back = value_back + jnp.pad(value_step, padding)
    query_turned = jnp.concatenate(query_back_parts, axis=0).reshape(length, 4, HEAD_SIZE)
    query_unturned = unrotate(query_turned, cosine, sine)
    query_gain_grad = jnp.sum(query_unturned * query_shaped, axis=(0, 1))
    d_query = (
        norm_back(query_unturned, query_shaped, query_inverse, query_gain)
        .reshape(length, 512)
        .astype(bf)
    )
    key_unturned = unrotate(key_back, cosine, sine)
    key_gain_grad = jnp.sum(key_unturned * key_shaped, axis=(0, 1))
    d_key = (
        norm_back(key_unturned, key_shaped, key_inverse, key_gain).reshape(length, 256).astype(bf)
    )
    d_value = value_back.reshape(length, 256).astype(bf)
    grad_query = dot(rows_one, d_query, ((0,), (0,)))
    grad_key = dot(rows_one, d_key, ((0,), (0,)))
    grad_value = dot(rows_one, d_value, ((0,), (0,)))
    first_part = (
        dot(d_query, wq, ((1,), (1,))) + dot(d_key, wk, ((1,), (1,))) + dot(d_value, wv, ((1,), (1,)))
    )
    one_share = scatter_sum(first_part.astype(bf).reshape(2, 4, 128, width), "z", z, 1)
    attn_gain_grad = jnp.sum(one_share * normed_one, axis=(0, 1))
    input_grad = middle_grad + norm_back(one_share, normed_one, inverse_one, attn_gain)

    gain_grad = jnp.concatenate([attn_gain_grad, feed_gain_grad, query_gain_grad, key_gain_grad])
    gain_parts = jnp.broadcast_to(gain_grad.reshape(16, 1, 144), (16, 8, 144)).reshape(128, 144)
    gain_sum = jnp.sum(lax.all_to_all(gain_parts, ALL, 0, 0, tiled=True), axis=0)

    rest_grad = jnp.concatenate(
        [
            grad_out.reshape(width, 2, 256),
            grad_gate.reshape(width, 2, 384),
            grad_up.reshape(width, 2, 384),
            grad_down.reshape(width, 2, 384),
        ],
        axis=2,
    )
    rest_sum = scatter_weight(rest_grad, c)
    attn_grad = jnp.concatenate(
        [
            grad_query.reshape(width, 2, 256),
            grad_key.reshape(width, 2, 128),
            grad_value.reshape(width, 2, 128),
        ],
        axis=2,
    )
    attn_sum = scatter_weight(attn_grad, c)

    result = by_sequence(result, xl)
    input_grad = by_sequence(input_grad, xl)

    wide_rate = matrix_rate * MODEL_WIDTH ** (-0.5)
    updates = (
        adamw(query_weight, query_first, query_second, attn_sum[:, :256], wide_rate)
        + adamw(key_weight, key_first, key_second, attn_sum[:, 256:384], wide_rate)
        + adamw(value_weight, value_first, value_second, attn_sum[:, 384:], wide_rate)
        + adamw(
            out_weight, out_first, out_second, rest_sum[:, :256].T, matrix_rate * WO_FAN ** (-0.5)
        )
        + adamw(gate_weight, gate_first, gate_second, rest_sum[:, 256:640], wide_rate)
        + adamw(up_weight, up_first, up_second, rest_sum[:, 640:1024], wide_rate)
        + adamw(
            down_weight, down_first, down_second, rest_sum[:, 1024:].T, matrix_rate * FF ** (-0.5)
        )
        + adamw(gains, gain_first, gain_second, gain_sum, gain_rate)
    )
    return (result, input_grad) + updates


def solution(mesh):
    split = Mesh(mesh.devices.reshape(2, 4, 2, 2, 4), ALL)
    rows = P(DP, TENSOR, None)
    wide = (P(DP, TENSOR),) * 3
    tall = (P(TENSOR, DP),) * 3
    flat = (P(DP),) * 3
    weights = wide * 3 + tall + wide * 2 + tall + flat
    return jax.shard_map(
        per_device,
        mesh=split,
        in_specs=(rows, P(DP, None), rows) + weights,
        out_specs=(rows, rows) + weights,
        check_vma=False,
    )
```

```python
import functools
import math

import jax
import jax.numpy as jnp
from jax import lax
from jax.experimental import pallas as pl
from jax.experimental.pallas import tpu as pltpu
from jax.sharding import Mesh
from jax.sharding import PartitionSpec as P

MODEL_WIDTH = 1024
QUERY_HEADS = 16
KEY_VALUE_HEADS = 8
HEAD_SIZE = 128
FF = 3072
STEP = 10
WO_FAN = 40

norm_eps = 1e-06
rope_base = 1000000.0
beta_one = 0.9
beta_two = 0.95
adam_eps = 1e-08
decay_rate = 0.1
matrix_rate = 2.5
gain_rate = 0.5
doc_limit = 3

bf = jnp.bfloat16
f32 = jnp.float32
X = ("xh", "xl")
ALL = ("xh", "y", "c", "xl", "z")
DP = ("xh", "y", "c")
TENSOR = ("xl", "z")


SCORE = HEAD_SIZE ** (-0.5)
EXPONENT = SCORE / math.log(2.0)
VMEM = pl.BlockSpec(memory_space=pltpu.VMEM)
SMEM = pl.BlockSpec(memory_space=pltpu.SMEM)
LIMIT = 24 * 1024 * 1024
GAIN_AT = 6 * 64
ATTN_ROWS = GAIN_AT + 32
FEED_ROWS = 9 * 64


COST = pl.CostEstimate(flops=1, bytes_accessed=1, transcendentals=0)


def params(limit=LIMIT):
    return pltpu.CompilerParams(vmem_limit_bytes=limit)


def struct(shape, dtype=bf):
    return jax.ShapeDtypeStruct(shape, dtype)


def dot(left, right, dims):
    return lax.dot_general(left, right, (dims, ((), ())), preferred_element_type=f32)


NN = ((1,), (0,))
NT = ((1,), (1,))
TN = ((0,), (0,))


def rms_parts(rows):
    inverse = lax.rsqrt(jnp.mean(rows * rows, axis=-1, keepdims=True) + norm_eps)
    return (rows * inverse, inverse)


def norm_back(grad, scaled, inverse, gain):
    pushed = grad * gain
    return inverse * (pushed - scaled * jnp.mean(pushed * scaled, axis=-1, keepdims=True))


def positions(segment):
    before = jnp.zeros(segment.shape, jnp.int32)
    for level in range(doc_limit):
        count = jnp.sum((segment == level).astype(jnp.int32), axis=-1, keepdims=True)
        before = before + jnp.where(segment > level, count, 0)
    return lax.broadcasted_iota(jnp.int32, segment.shape, segment.ndim - 1) - before


def rope_tables(segment, width):
    place = positions(segment)
    start = jnp.arange(segment.shape[0], dtype=jnp.int32) - place
    place = place.astype(f32)
    index = jnp.arange(width // 2, dtype=f32)
    inverse = jnp.exp(index * (-2.0 * math.log(rope_base) / width))
    angle = place[..., None] * inverse
    cosine = jnp.cos(angle)
    sine = jnp.sin(angle)
    cosine = jnp.concatenate([cosine, cosine], axis=-1)
    sine = jnp.concatenate([-sine, sine], axis=-1)
    return cosine, sine, start[None, :]


def ring(count, step):
    return [(i, (i + step) % count) for i in range(count)]


def swap(value, axis):
    return lax.ppermute(value, axis, ring(2, 1))


def fetch(value, axis):
    far = lax.ppermute(value, axis, ring(4, 2))
    left = lax.ppermute(value, axis, ring(4, 1))
    right = lax.ppermute(value, axis, ring(4, 3))
    return [value, left, far, right]


def spread(parts, axis):
    far = lax.ppermute(parts[2], axis, ring(4, 2))
    left = lax.ppermute(parts[1], axis, ring(4, 1))
    right = lax.ppermute(parts[3], axis, ring(4, 3))
    return [parts[0], left, far, right]


def total(parts):
    return sum(part.astype(f32) for part in parts)


def after(value, *others):
    return lax.optimization_barrier((value, others))[0]


def by_sequence(value, xl, sent=None):
    keep = lax.dynamic_index_in_dim(value, xl, 0, keepdims=False)
    other = lax.dynamic_index_in_dim(value, 1 - xl, 0, keepdims=False)
    other = swap(other if sent is None else other.astype(sent), "xl").astype(value.dtype)
    first = xl == 0
    return jnp.stack([jnp.where(first, keep, other), jnp.where(first, other, keep)])


def adamw(weight, first, second, grad, rate):
    first_new = beta_one * first + (1.0 - beta_one) * grad
    second_new = beta_two * second + (1.0 - beta_two) * grad * grad
    ratio = (
        first_new
        / (1.0 - beta_one**STEP)
        / (jnp.sqrt(second_new / (1.0 - beta_two**STEP)) + adam_eps)
    )
    return (weight - rate * (ratio + decay_rate * weight), first_new, second_new)


def place_rows(pack, core, y, target, block, column):
    for xh in range(2):
        for j in range(4):
            at = pl.multiple_of((xh * 4 + lax.rem(y + 4 - j, 4)) * 128 + core * 64, 64)
            for xl in range(2):
                target[pl.ds(at, 64), column(xl) : column(xl) + 128] = pack[
                    xh * 2 + xl, j, block * 64 : block * 64 + 64, :
                ]


def qkv_kernel(
    info, n0, n1, n2, n3, mine, other, cosine, sine,
    h1, q_raw, k_raw, q_rot, k_rot, v_out, weight, weight_out, gain_out,
):
    z, c, y = info[0], info[1], info[3]
    gain = jnp.zeros((32, 128), f32)
    for pack, core in ((mine, c), (other, 1 - c)):
        place_rows(pack, core, y, weight, 0, lambda xl: xl * 256)
        place_rows(pack, core, y, weight, 1, lambda xl: xl * 256 + 128)
        place_rows(pack, core, y, weight, 2, lambda xl: xl * 128 + 512)
        place_rows(pack, core, y, weight, 3, lambda xl: xl * 128 + 768)
        place_rows(pack, core, y, weight_out, 4, lambda xl: xl * 256)
        place_rows(pack, core, y, weight_out, 5, lambda xl: xl * 256 + 128)
        for i in range(4):
            for j in range(4):
                gain += pack[i, j, GAIN_AT:ATTN_ROWS, :].astype(f32)
    gain = gain * 0.5
    gain_out[...] = gain
    for step, chunk in enumerate((n0, n1, n2, n3)):
        at = lax.rem(z + 4 - step, 4)
        rows = chunk[...].reshape(256, MODEL_WIDTH)
        rows = jnp.concatenate(
            [
                (rows[:, j * 128 : j * 128 + 128].astype(f32) * gain[j : j + 1, :]).astype(bf)
                for j in range(8)
            ],
            axis=1,
        )
        h1[:, at] = rows.reshape(2, 128, MODEL_WIDTH)
        made = dot(rows, weight[...], NN)
        cos = cosine[:, at].reshape(256, HEAD_SIZE)
        sin = sine[:, at].reshape(256, HEAD_SIZE)
        q_raw[:, at] = made[:, :512].reshape(2, 128, 512)
        k_raw[:, at] = made[:, 512:768].reshape(2, 128, 256)
        v_out[:, at] = made[:, 768:].astype(bf).reshape(2, 128, 256)
        for head in range(6):
            raw = made[:, head * 128 : head * 128 + 128]
            scaled, _ = rms_parts(raw)
            scaled = scaled * (gain[16:17, :] if head < 4 else gain[17:18, :])
            turned = scaled * cos + pltpu.roll(scaled, 64, 1) * sin
            if head < 4:
                turned = turned * EXPONENT
                q_rot[:, at, :, head * 128 : head * 128 + 128] = turned.astype(bf).reshape(2, 128, 128)
            else:
                to = (head - 4) * 128
                k_rot[:, at, :, to : to + 128] = turned.astype(bf).reshape(2, 128, 128)


def allowed(start_row, i, j):
    key = lax.broadcasted_iota(jnp.int32, (256, 256), 0) + 256 * j
    seen = key >= start_row
    if i == j:
        seen = seen & (key <= lax.broadcasted_iota(jnp.int32, (256, 256), 1) + 256 * i)
    return seen


def attention_kernel(q_rot, k_rot, v_in, start, out, total_log):
    v_turned = v_in[...].T
    for i in range(4):
        rows = slice(256 * i, 256 * i + 256)
        q = q_rot[rows, :]
        total = jnp.zeros((1, 256), f32)
        o = jnp.zeros((HEAD_SIZE, 256), f32)
        for j in range(i + 1):
            keys = slice(256 * j, 256 * j + 256)
            s = dot(k_rot[keys, :], q, NT)
            p = jnp.where(allowed(start[:, rows], i, j), jnp.exp2(s), 0.0)
            total += jnp.sum(p, axis=0, keepdims=True)
            o += dot(v_turned[:, keys], p.astype(bf), NN)
        out[rows, :] = (o / total).T.astype(bf)
        total_log[0, :, rows] = jnp.log2(total)


def attention_back_kernel(
    q_rot, k_rot, v_in, o_in, d_o, total_log, q_raw, k_raw, cosine, sine, gain_q, gain_k, start,
    d_q, d_k, d_v, gain_grad, dk_sum, dv_sum,
):
    q_gain_sum = jnp.zeros((1, HEAD_SIZE), f32)
    k_turned = k_rot[...].T
    for r in range(2):
        cols = slice(r * 128, r * 128 + 128)
        for i in (3, 2, 1, 0):
            rows = slice(256 * i, 256 * i + 256)
            q = q_rot[rows, cols]
            push = d_o[rows, cols]
            centre = jnp.sum(
                (push.astype(f32) * o_in[rows, cols].astype(f32)).T, axis=0, keepdims=True
            )
            shift = total_log[r, :, rows]
            grad = jnp.zeros((HEAD_SIZE, 256), f32)
            for j in range(i + 1):
                keys = slice(256 * j, 256 * j + 256)
                s = dot(k_rot[keys, :], q, NT)
                p = jnp.where(allowed(start[:, rows], i, j), jnp.exp2(s - shift), 0.0)
                d_p = dot(v_in[keys, :], push, NT)
                d_s = (p * (d_p - centre)).astype(bf)
                part_k = dot(d_s, q, NN)
                part_v = dot(p.astype(bf), push, NN)
                if r == 0 and i == 3:
                    dk_sum[keys, :] = part_k
                    dv_sum[keys, :] = part_v
                else:
                    dk_sum[keys, :] += part_k
                    dv_sum[keys, :] += part_v
                grad += dot(k_turned[:, keys], d_s, NN)
            grad = grad.T * SCORE
            cos, sin = cosine[rows, :], sine[rows, :]
            grad = grad * cos - pltpu.roll(grad, 64, 1) * sin
            scaled, inverse = rms_parts(q_raw[rows, cols])
            q_gain_sum += jnp.sum(grad * scaled, axis=0, keepdims=True)
            d_q[rows, cols] = norm_back(grad, scaled, inverse, gain_q[...]).astype(bf)
    grad = dk_sum[...] * (SCORE / EXPONENT)
    grad = grad * cosine[...] - pltpu.roll(grad, 64, 1) * sine[...]
    scaled, inverse = rms_parts(k_raw[...])
    d_k[...] = norm_back(grad, scaled, inverse, gain_k[...]).astype(bf)
    d_v[...] = dv_sum[...].astype(bf)
    gain_grad[0] = jnp.concatenate(
        [q_gain_sum, jnp.sum(grad * scaled, axis=0, keepdims=True), jnp.zeros((6, HEAD_SIZE), f32)], axis=0
    )


def parts_kernel(count, info, *refs):
    lefts, weight, outs = refs[:count], refs[count], refs[count + 1 :]
    for k in (2, 1, 3, 0):
        at = lax.rem(info[0] + k, 4)
        total = None
        column = 0
        for left in lefts:
            n = left.shape[-1]
            part = dot(left[:, at].reshape(256, n), weight[:, column : column + n], NT)
            total = part if total is None else total + part
            column += n
        outs[k][...] = total.astype(bf).reshape(2, 128, MODEL_WIDTH)


def send_parts(info, lefts, weight):
    return pl.pallas_call(
        functools.partial(parts_kernel, len(lefts)),
        out_shape=[struct((2, 128, MODEL_WIDTH))] * 4,
        in_specs=[SMEM] + [VMEM] * (len(lefts) + 1),
        out_specs=[VMEM] * 4,
        compiler_params=params(),
        cost_estimate=COST,
    )(info, *[left.reshape(2, 4, 128, left.shape[-1]) for left in lefts], weight)


def back_out_kernel(info, m0, m1, m2, m3, weight_out, d_o):
    for step, chunk in enumerate((m0, m1, m2, m3)):
        at = lax.rem(info[0] + 4 - step, 4)
        d_o[:, at] = dot(chunk[...].reshape(256, MODEL_WIDTH), weight_out[...], NN).astype(bf).reshape(2, 128, 512)


def feed_weights_kernel(info, mine, other, gate, up, down):
    c, y = info[1], info[3]
    for pack, core in ((mine, c), (other, 1 - c)):
        for number, target in enumerate((gate, up, down)):
            for j in range(3):
                place_rows(pack, core, y, target, number * 3 + j, lambda xl, j=j: xl * 384 + j * 128)


def feed_kernel(rows_ref, push_ref, gate_w, up_w, down_w, out, d_rows, hidden_out, d_gate_out, d_up_out):
    rows = rows_ref[...].reshape(256, MODEL_WIDTH)
    push = push_ref[...].reshape(256, MODEL_WIDTH)
    total = jnp.zeros((256, MODEL_WIDTH), f32)
    back = jnp.zeros((256, MODEL_WIDTH), f32)
    for j in range(3):
        cols = slice(j * 256, j * 256 + 256)
        gate = dot(rows, gate_w[:, cols], NN)
        up = dot(rows, up_w[:, cols], NN)
        d_hidden = dot(push, down_w[:, cols], NN)
        sigma = jax.nn.sigmoid(gate)
        swish = gate * sigma
        hidden = (swish * up).astype(bf)
        d_gate = (d_hidden * up * (sigma + swish * (1.0 - sigma))).astype(bf)
        d_up = (d_hidden * swish).astype(bf)
        hidden_out[:, cols] = hidden
        d_gate_out[:, cols] = d_gate
        d_up_out[:, cols] = d_up
        total += dot(hidden, down_w[:, cols], NT)
        back += dot(d_gate, gate_w[:, cols], NT) + dot(d_up, up_w[:, cols], NT)
    out[...] = total.astype(bf).reshape(2, 128, MODEL_WIDTH)
    d_rows[...] = back.astype(bf).reshape(2, 128, MODEL_WIDTH)


def feed_chunk(rows, push, weights):
    return pl.pallas_call(
        feed_kernel,
        out_shape=[struct((2, 128, MODEL_WIDTH))] * 2 + [struct((256, 768))] * 3,
        in_specs=[VMEM] * 5,
        out_specs=[VMEM] * 5,
        compiler_params=params(),
        cost_estimate=COST,
    )(rows, push, *weights)


def put_blocks(grad, base, count, per, core, keep, send):
    for yy in range(2):
        low = grad[yy * 128 : yy * 128 + 64].astype(bf)
        high = grad[yy * 128 + 64 : yy * 128 + 128].astype(bf)
        first = core == 0
        mine = jnp.where(first, low, high)
        other = jnp.where(first, high, low)
        for xl in range(2):
            for j in range(count):
                at = slice((base + j) * 64, (base + j) * 64 + 64)
                cols = slice(xl * per + j * 128, xl * per + j * 128 + 128)
                keep[xl, yy, at, :] = mine[:, cols]
                send[xl, yy, at, :] = other[:, cols]


def feed_grad_kernel(info, *refs):
    rows, push, hidden, d_gate, d_up = refs[:4], refs[4:8], refs[8:12], refs[12:16], refs[16:20]
    keep, send = refs[20:]
    for number, (lefts, rights) in enumerate(((rows, d_gate), (rows, d_up), (push, hidden))):
        total = None
        for left, right in zip(lefts, rights):
            part = dot(left[...].reshape(256, 256), right[...], TN)
            total = part if total is None else total + part
        put_blocks(total, number * 3, 3, 384, info[1], keep, send)


def grad_spec(rows):
    return pl.BlockSpec((2, 2, rows, 128), lambda i: (i // 2, i % 2, 0, 0))


def feed_grads(info, rows, push, hidden, d_gate, d_up):
    narrow = pl.BlockSpec((2, 128, 256), lambda i: (0, 0, i))
    whole = pl.BlockSpec((256, 768), lambda i: (0, 0))
    return pl.pallas_call(
        feed_grad_kernel,
        grid=(4,),
        out_shape=[struct((4, 4, FEED_ROWS, 128))] * 2,
        in_specs=[SMEM] + [narrow] * 8 + [whole] * 12,
        out_specs=[grad_spec(FEED_ROWS)] * 2,
        compiler_params=params(),
        cost_estimate=COST,
    )(info, *rows, *push, *hidden, *d_gate, *d_up)


def attn_grad_kernel(
    info, rows, d_q, d_k, d_v, weight, m0, m1, m2, m3, mixed, keep, send, gain_grad
):
    left = rows[...]
    total = jnp.zeros((256, 1), f32)
    for grad_ref, base, count, per, column in ((d_q, 0, 2, 256, 0), (d_k, 2, 1, 128, 512), (d_v, 3, 1, 128, 768)):
        grad = dot(left, grad_ref[...], TN)
        put_blocks(grad, base, count, per, info[1], keep, send)
        against = weight[:, column : column + 2 * per].astype(f32)
        total += jnp.sum(grad * against, axis=1, keepdims=True)
    gain_grad[...] = total
    grad = None
    for step, chunk in enumerate((m0, m1, m2, m3)):
        at = lax.rem(info[0] + 4 - step, 4)
        part = dot(chunk[...].reshape(256, 256), mixed[:, at].reshape(256, 512), TN)
        grad = part if grad is None else grad + part
    put_blocks(grad, 4, 2, 256, info[1], keep, send)


def attn_grads(info, rows, d_q, d_k, d_v, weight, chunks, mixed):
    length = rows.shape[0]
    return pl.pallas_call(
        attn_grad_kernel,
        grid=(4,),
        out_shape=[struct((4, 4, GAIN_AT, 128))] * 2 + [struct((MODEL_WIDTH, 1), f32)],
        in_specs=[SMEM, pl.BlockSpec((length, 256), lambda i: (0, i))]
        + [pl.BlockSpec((length, n), lambda i: (0, 0)) for n in (512, 256, 256)]
        + [pl.BlockSpec((256, MODEL_WIDTH), lambda i: (i, 0))]
        + [pl.BlockSpec((2, 128, 256), lambda i: (0, 0, i))] * 4
        + [pl.BlockSpec((2, 4, 128, 512), lambda i: (0, 0, 0, 0))],
        out_specs=[grad_spec(GAIN_AT)] * 2 + [pl.BlockSpec((256, 1), lambda i: (i, 0))],
        compiler_params=params(),
        cost_estimate=COST,
    )(info, rows, d_q, d_k, d_v, weight, *chunks, mixed.reshape(2, 4, 128, 512))


def pack_kernel(query, key, value, out, slots, gate, up, down, pack, *scratch):
    sources = (query, key, value, out, slots, gate, up, down)
    held, sems = scratch[:-1], scratch[-1]
    copies = [pltpu.make_async_copy(a, b, sems.at[n]) for n, (a, b) in enumerate(zip(sources, held))]
    for copy in copies:
        copy.start()
    at = 0
    for copy, block in zip(copies, held):
        copy.wait()
        rows = block.shape[0]
        for j in range(0, block.shape[1], 128):
            pack[at : at + rows, :] = block[:, j : j + 128].astype(bf)
            at += rows


def pack_weights(sources):
    return pl.pallas_call(
        pack_kernel,
        out_shape=struct((ATTN_ROWS + FEED_ROWS, 128)),
        in_specs=[pl.BlockSpec(memory_space=pl.ANY)] * len(sources),
        out_specs=VMEM,
        scratch_shapes=[pltpu.VMEM(a.shape, a.dtype) for a in sources] + [pltpu.SemaphoreType.DMA((len(sources),))],
        compiler_params=params(),
        cost_estimate=COST,
    )(*sources)


def split_kernel(at, info, *refs):
    sources, outs = refs[:-4], refs[-4:]
    for k in range(4):
        place = lax.rem(info[at] + k, 4)
        total = sources[0][place].astype(f32)
        for source in sources[1:]:
            total += source[place].astype(f32)
        outs[k][...] = total.astype(bf)


def split(info, at, *sources):
    return pl.pallas_call(
        functools.partial(split_kernel, at),
        out_shape=[struct(sources[0].shape[1:])] * 4,
        in_specs=[SMEM] + [VMEM] * len(sources),
        out_specs=[VMEM] * 4,
        compiler_params=params(),
        cost_estimate=COST,
    )(info, *sources)


def adam_kernel(rates, n_parts, *refs):
    grads, refs = refs[:n_parts], refs[n_parts:]
    states, outs = refs[: 3 * len(rates)], refs[3 * len(rates) :]
    at = 0
    for n, rate in enumerate(rates):
        for j in range(0, states[3 * n].shape[1], 128):
            grad = grads[0][at : at + 64, :].astype(f32)
            for other in grads[1:]:
                grad += other[at : at + 64, :].astype(f32)
            cols = slice(j, j + 128)
            made = adamw(*[ref[:, cols] for ref in states[3 * n : 3 * n + 3]], grad, rate)
            for ref, value in zip(outs[3 * n : 3 * n + 3], made):
                ref[:, cols] = value
            at += 64


def adam(parts, states, rates):
    return pl.pallas_call(
        functools.partial(adam_kernel, rates, len(parts)),
        out_shape=[struct(a.shape, f32) for a in states],
        in_specs=[VMEM] * (len(parts) + len(states)),
        out_specs=[VMEM] * len(states),
        compiler_params=params(),
        cost_estimate=COST,
    )(*parts, *states)


def per_device(
    inputs,
    segments,
    cotangent,
    query_weight,
    query_first,
    query_second,
    key_weight,
    key_first,
    key_second,
    value_weight,
    value_first,
    value_second,
    out_weight,
    out_first,
    out_second,
    gate_weight,
    gate_first,
    gate_second,
    up_weight,
    up_first,
    up_second,
    down_weight,
    down_first,
    down_second,
    gains,
    gain_first,
    gain_second,
):
    width = inputs.shape[2]
    length = segments.shape[1]
    xl, z, y, c = (lax.axis_index(name) for name in ("xl", "z", "y", "c"))
    x = lax.axis_index(X)
    info = jnp.stack([z, c, x, y]).astype(jnp.int32)
    place = (x // 2 * 4 + y) * 2 + c

    both = by_sequence(jnp.concatenate([inputs, cotangent], axis=2), xl)
    gain_slots = lax.dynamic_update_slice(jnp.zeros((32 * 128,), bf), gains.astype(bf), (place * 144,))
    pack = pack_weights(
        (query_weight, key_weight, value_weight, out_weight.T, gain_slots.reshape(32, 128))
        + (gate_weight, up_weight, down_weight.T)
    )
    packs, both = lax.optimization_barrier((fetch(pack, "y"), both))
    base, push = both[..., :width], both[..., width:]

    base = base.astype(f32)
    normed_one, inverse_one = rms_parts(base)
    sent_one = normed_one.astype(bf)
    rows_one = fetch(sent_one, "z")
    attn_rows = lax.all_gather(jnp.stack([p[:ATTN_ROWS] for p in packs]), X)
    attn_rows, rows_one = lax.optimization_barrier((attn_rows, rows_one))
    attn_other = swap(attn_rows, "c")
    push_all = fetch(after(push, rows_one), "z")
    feed_rows = lax.all_gather(after(jnp.stack([p[ATTN_ROWS:] for p in packs]), attn_rows), X)

    segment = lax.dynamic_index_in_dim(segments, xl, 0, keepdims=False)
    cosine, sine, start = rope_tables(segment, HEAD_SIZE)

    h1, q_raw, k_raw, q_rot, k_rot, value, w_qkv, w_out, gain_all = pl.pallas_call(
        qkv_kernel,
        out_shape=[
            struct((2, 4, 128, width)),
            struct((2, 4, 128, 512), f32),
            struct((2, 4, 128, 256), f32),
            struct((2, 4, 128, 512)),
            struct((2, 4, 128, 256)),
            struct((2, 4, 128, 256)),
            struct((width, 1024)),
            struct((width, 512)),
            struct((32, 128), f32),
        ],
        in_specs=[SMEM] + [VMEM] * 8,
        out_specs=[VMEM] * 9,
        compiler_params=params(),
        cost_estimate=COST,
    )(
        info,
        *rows_one,
        attn_rows,
        attn_other,
        cosine.reshape(2, 4, 128, HEAD_SIZE),
        sine.reshape(2, 4, 128, HEAD_SIZE),
    )
    attn_gain = gain_all[:8].reshape(1, width)
    feed_gain = gain_all[8:16].reshape(1, width)
    query_gain = gain_all[16:17]
    key_gain = gain_all[17:18]
    q_raw, q_rot = (a.reshape(length, 512) for a in (q_raw, q_rot))
    k_raw, k_rot, value = (a.reshape(length, 256) for a in (k_raw, k_rot, value))
    head = pl.BlockSpec((length, 128), lambda h: (0, h))
    group = pl.BlockSpec((length, 128), lambda h: (0, h // 2))
    row_spec = pl.BlockSpec((1, length), lambda h: (0, 0))
    mixed, total_log = pl.pallas_call(
        attention_kernel,
        grid=(4,),
        out_shape=[struct((length, 512)), struct((4, 1, length), f32)],
        in_specs=[head, group, group, row_spec],
        out_specs=[head, pl.BlockSpec((1, 1, length), lambda h: (h, 0, 0))],
        compiler_params=params(),
        cost_estimate=COST,
    )(q_rot, k_rot, value, start)

    mixed, push_all = lax.optimization_barrier((mixed, push_all))
    feed_rows = after(feed_rows, mixed)
    feed_other = swap(feed_rows, "c")
    middle = base + total(spread(send_parts(info, [mixed], w_out), "z"))
    normed_two, inverse_two = rms_parts(middle)
    feed_weights = pl.pallas_call(
        feed_weights_kernel,
        out_shape=[struct((width, 768))] * 3,
        in_specs=[SMEM, VMEM, VMEM],
        out_specs=[VMEM] * 3,
        compiler_params=params(),
        cost_estimate=COST,
    )(info, feed_rows, feed_other)
    rows_two = fetch((normed_two * feed_gain).astype(bf), "z")
    own = feed_chunk(rows_two[0], push_all[0], feed_weights)
    left = feed_chunk(after(rows_two[1], own), push_all[1], feed_weights)
    right = feed_chunk(after(rows_two[3], left), push_all[3], feed_weights)
    two_left = lax.ppermute(left[1], "z", ring(4, 3))
    far = feed_chunk(after(rows_two[2], right, two_left), push_all[2], feed_weights)
    two_far = lax.ppermute(far[1], "z", ring(4, 2))
    two_right = lax.ppermute(right[1], "z", ring(4, 1))
    two_share = total([own[1], two_left, two_right, two_far])
    outs, _, hiddens, d_gates, d_ups = zip(own, left, far, right)
    feed_keep, feed_send = feed_grads(info, rows_two, push_all, hiddens, d_gates, d_ups)
    feed_gain_grad = jnp.sum(two_share * normed_two, axis=(0, 1))
    middle_grad = push.astype(f32) + norm_back(two_share, normed_two, inverse_two, feed_gain)
    sent_middle = middle_grad.astype(bf)
    mixed_rows = fetch(sent_middle, "z")
    feed_sum = swap(after(feed_send, two_right), "c").astype(f32) + after(feed_keep, mixed_rows[1]).astype(f32)
    feed_sum = feed_sum.astype(bf)
    feed_sum = lax.psum_scatter(feed_sum, X, scatter_dimension=0, tiled=False)
    outs = after(outs, mixed_rows)
    out_parts = spread([outs[0], outs[3], outs[2], outs[1]], "z")
    d_o = pl.pallas_call(
        back_out_kernel,
        out_shape=struct((2, 4, 128, 512)),
        in_specs=[SMEM] + [VMEM] * 5,
        out_specs=VMEM,
        compiler_params=params(),
        cost_estimate=COST,
    )(info, *mixed_rows, w_out).reshape(length, 512)

    pair = pl.BlockSpec((length, 256), lambda g: (0, g))
    one = pl.BlockSpec((length, 128), lambda g: (0, g))
    table = pl.BlockSpec((length, 128), lambda g: (0, 0))
    row = pl.BlockSpec((1, 128), lambda g: (0, 0))
    d_q, d_k, d_v, head_gain_grads = pl.pallas_call(
        attention_back_kernel,
        grid=(2,),
        out_shape=[struct((length, 512)), struct((length, 256)), struct((length, 256)), struct((2, 8, 128), f32)],
        in_specs=[pair, one, one, pair, pair, pl.BlockSpec((2, 1, length), lambda g: (g, 0, 0)), pair, one]
        + [table, table, row, row, row_spec],
        out_specs=[pair, one, one, pl.BlockSpec((1, 8, 128), lambda g: (g, 0, 0))],
        scratch_shapes=[pltpu.VMEM((length, 128), f32)] * 2,
        compiler_params=params(),
        cost_estimate=COST,
    )(q_rot, k_rot, value, mixed, d_o, total_log, q_raw, k_raw, cosine, sine, query_gain, key_gain, start)

    feed_sum, d_q, out_parts = lax.optimization_barrier((feed_sum, d_q, out_parts))
    feed_sum = lax.psum_scatter(feed_sum, "y", scatter_dimension=0, tiled=False)
    one_parts = send_parts(info, [d_q, d_k, d_v], w_qkv)
    one_share = spread(one_parts, "z")
    d_q, d_k, d_v = after((d_q, d_k, d_v), one_parts)
    attn_keep, attn_send, attn_gain_grad = attn_grads(
        info, h1.reshape(length, width), d_q, d_k, d_v, w_qkv, mixed_rows, mixed
    )
    result = by_sequence((middle + total(out_parts)).astype(bf), xl)
    attn_send = after(attn_send, one_share[1], result)
    x_parts = spread(split(info, 2, attn_keep, swap(attn_send, "c")), X)
    one_share = total(after(one_share, x_parts[1]))
    input_grad = middle_grad + norm_back(one_share, normed_one, inverse_one, attn_gain)
    input_grad = by_sequence(input_grad, xl, bf)
    attn_gain_grad = (attn_gain_grad.reshape(1, width) / attn_gain)[0]
    head_gain_grads = jnp.sum(head_gain_grads, axis=0)
    gain_grad = jnp.concatenate([attn_gain_grad, feed_gain_grad, head_gain_grads[0], head_gain_grads[1]])
    gain_parts = jnp.broadcast_to(gain_grad.reshape(16, 1, 144), (16, 8, 144)).reshape(128, 144)
    gain_sum = jnp.sum(lax.all_to_all(after(gain_parts, x_parts[1]), ALL, 0, 0, tiled=True), axis=0)
    y_parts = split(info, 3, *x_parts)
    feed_sum = after(feed_sum, y_parts)
    y_parts = spread(y_parts, "y")

    wide_rate = matrix_rate * MODEL_WIDTH ** (-0.5)
    gate_up_down = adam(
        [feed_sum],
        [gate_weight, gate_first, gate_second, up_weight, up_first, up_second]
        + [down_weight.T, down_first.T, down_second.T],
        (wide_rate, wide_rate, matrix_rate * FF ** (-0.5)),
    )
    attn_new = adam(
        y_parts,
        [query_weight, query_first, query_second, key_weight, key_first, key_second]
        + [value_weight, value_first, value_second, out_weight.T, out_first.T, out_second.T],
        (wide_rate, wide_rate, wide_rate, matrix_rate * WO_FAN ** (-0.5)),
    )
    gains_new = adamw(gains, gain_first, gain_second, gain_sum, gain_rate)
    updates = (*attn_new[:9], *[a.T for a in attn_new[9:]], *gate_up_down[:6], *[a.T for a in gate_up_down[6:]])
    return (result, input_grad, *updates, *gains_new)


def solution(mesh):
    split = Mesh(mesh.devices.reshape(2, 4, 2, 2, 4), ALL)
    rows = P(DP, TENSOR, None)
    wide = (P(DP, TENSOR),) * 3
    tall = (P(TENSOR, DP),) * 3
    flat = (P(DP),) * 3
    weights = wide * 3 + tall + wide * 2 + tall + flat
    return jax.shard_map(
        per_device,
        mesh=split,
        in_specs=(rows, P(DP, None), rows) + weights,
        out_specs=(rows, rows) + weights,
        check_vma=False,
    )
```

```python
import functools
import math

import jax
import jax.numpy as jnp
from jax import lax
from jax.experimental import pallas as pl
from jax.experimental.pallas import tpu as pltpu
from jax.sharding import Mesh
from jax.sharding import PartitionSpec as P

MODEL_WIDTH = 1024
QUERY_HEADS = 16
KEY_VALUE_HEADS = 8
HEAD_SIZE = 128
FF = 3072
STEP = 10
WO_FAN = 40

norm_eps = 1e-06
rope_base = 1000000.0
beta_one = 0.9
beta_two = 0.95
adam_eps = 1e-08
decay_rate = 0.1
matrix_rate = 2.5
gain_rate = 0.5
doc_limit = 3

bf = jnp.bfloat16
f32 = jnp.float32
X = ("xh", "xl")
ALL = ("xh", "y", "c", "xl", "z")
DP = ("xh", "y", "c")
TENSOR = ("xl", "z")


SCORE = HEAD_SIZE ** (-0.5)
EXPONENT = SCORE / math.log(2.0)
VMEM = pl.BlockSpec(memory_space=pltpu.VMEM)
SMEM = pl.BlockSpec(memory_space=pltpu.SMEM)
HBM = pl.BlockSpec(memory_space=pltpu.HBM)
LIMIT = 50 * 1024 * 1024
FEED_LIMIT = 24 * 1024 * 1024
GAIN_AT = 6 * 64
ATTN_ROWS = GAIN_AT + 32
FEED_ROWS = 9 * 64


COST = pl.CostEstimate(flops=1, bytes_accessed=1, transcendentals=0)


def params(limit=LIMIT):
    return pltpu.CompilerParams(vmem_limit_bytes=limit)


class Staged:
    def __init__(self, source, buffer, sem):
        self.buffer, self.copy = buffer, pltpu.make_async_copy(source, buffer, sem)
        self.shape = buffer.shape
        self.copy.start()

    def __getitem__(self, at):
        if self.copy is not None:
            self.copy.wait()
            self.copy = None
        return self.buffer[at]


def staged_kernel(kernel, n_head, n_in, n_out, *refs):
    head, sources = refs[:n_head], refs[n_head : n_head + n_in]
    targets = refs[n_head + n_in : n_head + n_in + n_out]
    buffers = refs[n_head + n_in + n_out : n_head + 2 * n_in + n_out]
    outs, sems = refs[n_head + 2 * n_in + n_out : -1], refs[-1]
    kernel(*head, *[Staged(a, b, sems.at[n]) for n, (a, b) in enumerate(zip(sources, buffers))], *outs)
    stores = [pltpu.make_async_copy(a, b, sems.at[n_in + n]) for n, (a, b) in enumerate(zip(outs, targets))]
    for copy in stores:
        copy.start()
    for copy in stores:
        copy.wait()


def staged_call(kernel, out_shape, *inputs, info=None, resident=(), limit=LIMIT):
    head = () if info is None else (info,)
    n_in, n_out = len(inputs), len(out_shape)
    return pl.pallas_call(
        functools.partial(staged_kernel, kernel, len(head) + len(resident), n_in, n_out),
        out_shape=out_shape,
        in_specs=[SMEM] * len(head) + [VMEM] * len(resident) + [HBM] * n_in,
        out_specs=[HBM] * n_out,
        scratch_shapes=[pltpu.VMEM(a.shape, a.dtype) for a in (*inputs, *out_shape)]
        + [pltpu.SemaphoreType.DMA((n_in + n_out,))],
        compiler_params=params(limit),
        cost_estimate=COST,
    )(*head, *resident, *inputs)


def struct(shape, dtype=bf):
    return jax.ShapeDtypeStruct(shape, dtype)


def dot(left, right, dims):
    return lax.dot_general(left, right, (dims, ((), ())), preferred_element_type=f32)


NN = ((1,), (0,))
NT = ((1,), (1,))
TN = ((0,), (0,))


def rms_parts(rows):
    inverse = lax.rsqrt(jnp.mean(rows * rows, axis=-1, keepdims=True) + norm_eps)
    return (rows * inverse, inverse)


def norm_back(grad, scaled, inverse, gain):
    pushed = grad * gain
    return inverse * (pushed - scaled * jnp.mean(pushed * scaled, axis=-1, keepdims=True))


def positions(segment):
    before = jnp.zeros(segment.shape, jnp.int32)
    for level in range(doc_limit):
        count = jnp.sum((segment == level).astype(jnp.int32), axis=-1, keepdims=True)
        before = before + jnp.where(segment > level, count, 0)
    return lax.broadcasted_iota(jnp.int32, segment.shape, segment.ndim - 1) - before


def rope_tables(segment, width):
    place = positions(segment)
    start = jnp.arange(segment.shape[0], dtype=jnp.int32) - place
    place = place.astype(f32)
    index = jnp.arange(width // 2, dtype=f32)
    inverse = jnp.exp(index * (-2.0 * math.log(rope_base) / width))
    angle = place[..., None] * inverse
    cosine = jnp.cos(angle)
    sine = jnp.sin(angle)
    cosine = jnp.concatenate([cosine, cosine], axis=-1)
    sine = jnp.concatenate([-sine, sine], axis=-1)
    return cosine, sine, start[None, :]


def ring(count, step):
    return [(i, (i + step) % count) for i in range(count)]


def swap(value, axis):
    return lax.ppermute(value, axis, ring(2, 1))


def fetch(value, axis):
    far = lax.ppermute(value, axis, ring(4, 2))
    left = lax.ppermute(value, axis, ring(4, 1))
    right = lax.ppermute(value, axis, ring(4, 3))
    return [value, left, far, right]


def spread(parts, axis):
    far = lax.ppermute(parts[2], axis, ring(4, 2))
    left = lax.ppermute(parts[1], axis, ring(4, 1))
    right = lax.ppermute(parts[3], axis, ring(4, 3))
    return [parts[0], left, far, right]


def total(parts):
    return sum(part.astype(f32) for part in parts)


def after(value, *others):
    return lax.optimization_barrier((value, others))[0]


def by_sequence(value, xl):
    keep = lax.dynamic_index_in_dim(value, xl, 0, keepdims=False)
    other = swap(lax.dynamic_index_in_dim(value, 1 - xl, 0, keepdims=False), "xl")
    first = xl == 0
    return jnp.stack([jnp.where(first, keep, other), jnp.where(first, other, keep)])


def adamw(weight, first, second, grad, rate):
    first_new = beta_one * first + (1.0 - beta_one) * grad
    second_new = beta_two * second + (1.0 - beta_two) * grad * grad
    ratio = (
        first_new
        / (1.0 - beta_one**STEP)
        / (jnp.sqrt(second_new / (1.0 - beta_two**STEP)) + adam_eps)
    )
    return (weight - rate * (ratio + decay_rate * weight), first_new, second_new)


def place_rows(pack, core, y, target, block, column, halves=(0, 1)):
    for xh in range(2):
        for j in range(4):
            at = pl.multiple_of((xh * 4 + lax.rem(y + 4 - j, 4)) * 128 + core * 64, 64)
            for xl in halves:
                target[pl.ds(at, 64), column(xl) : column(xl) + 128] = pack[
                    xh * 2 + xl, j, block * 64 : block * 64 + 64, :
                ]


def allowed(start_row, i, j):
    key = lax.broadcasted_iota(jnp.int32, (256, 256), 0) + 256 * j
    seen = key >= start_row
    if i == j:
        seen = seen & (key <= lax.broadcasted_iota(jnp.int32, (256, 256), 1) + 256 * i)
    return seen


def position_rows(ref, at, cols=slice(None)):
    low = pl.multiple_of(at * 128, 128)
    return jnp.concatenate([ref[pl.ds(low, 128), cols], ref[pl.ds(low + 512, 128), cols]], axis=0)


def put_rows(ref, at, value, cols=slice(None)):
    low = pl.multiple_of(at * 128, 128)
    ref[pl.ds(low, 128), cols] = value[:128]
    ref[pl.ds(low + 512, 128), cols] = value[128:]


def forward_kernel(
    info, start, n0, n1, n2, n3, mine_in, other_in, cos_in, sin_in,
    q_raw_to, k_raw_to, q_rot_to, k_rot_to, v_to, weight_to, weight_out_to, mixed_to,
    far_to, left_to, right_to, own_to, gain_one, gain_two, gain_q, gain_k, total_log,
    mine, other, cosine, sine, rows_in, q_raw, k_raw, q_rot, k_rot, v_all, weight, weight_out, mixed,
    far, left, right, own, sems,
):
    z, c, y = info[0], info[1], info[3]
    pairs = [(mine_in, mine), (other_in, other), (cos_in, cosine), (sin_in, sine)]
    pairs += [(chunk, rows_in.at[n]) for n, chunk in enumerate((n0, n1, n2, n3))]
    copies = [pltpu.make_async_copy(a, b, sems.at[n]) for n, (a, b) in enumerate(pairs)]
    for copy in copies:
        copy.start()
    stores = []

    def store(source, target):
        copy = pltpu.make_async_copy(source, target, sems.at[8 + len(stores)])
        copy.start()
        stores.append(copy)

    gain = jnp.zeros((32, 128), f32)
    for copy, pack, core in ((copies[0], mine, c), (copies[1], other, 1 - c)):
        copy.wait()
        place_rows(pack, core, y, weight, 0, lambda xl: xl * 256)
        place_rows(pack, core, y, weight, 1, lambda xl: xl * 256 + 128)
        place_rows(pack, core, y, weight, 2, lambda xl: xl * 128 + 512)
        place_rows(pack, core, y, weight, 3, lambda xl: xl * 128 + 768)
        place_rows(pack, core, y, weight_out, 4, lambda xl: xl * 256)
        place_rows(pack, core, y, weight_out, 5, lambda xl: xl * 256 + 128)
        for i in range(4):
            for j in range(4):
                gain += pack[i, j, GAIN_AT:ATTN_ROWS, :].astype(f32)
    gain = gain * 0.5
    for j in range(8):
        gain_one[:, j * 128 : j * 128 + 128] = gain[j : j + 1, :]
        gain_two[:, j * 128 : j * 128 + 128] = gain[8 + j : 9 + j, :]
    gain_q[...] = gain[16:17, :]
    gain_k[...] = gain[17:18, :]
    store(weight, weight_to)
    store(weight_out, weight_out_to)
    copies[2].wait()
    copies[3].wait()
    for step in range(4):
        copies[4 + step].wait()
        at = lax.rem(z + 4 - step, 4)
        rows = rows_in[step].reshape(256, MODEL_WIDTH)
        rows = jnp.concatenate(
            [
                (rows[:, j * 128 : j * 128 + 128].astype(f32) * gain[j : j + 1, :]).astype(bf)
                for j in range(8)
            ],
            axis=1,
        )
        made = dot(rows, weight[...], NN)
        cos, sin = position_rows(cosine, at), position_rows(sine, at)
        put_rows(q_raw, at, made[:, :512].astype(bf))
        put_rows(k_raw, at, made[:, 512:768].astype(bf))
        put_rows(v_all, at, made[:, 768:].astype(bf))
        for head in range(6):
            cols = slice(head * 128, head * 128 + 128)
            scaled, _ = rms_parts(made[:, cols])
            scaled = scaled * (gain[16:17, :] if head < 4 else gain[17:18, :])
            turned = scaled * cos + pltpu.roll(scaled, 64, 1) * sin
            if head < 4:
                put_rows(q_rot, at, (turned * EXPONENT).astype(bf), cols)
            else:
                put_rows(k_rot, at, turned.astype(bf), slice(head * 128 - 512, head * 128 - 384))
    for source, target in ((q_raw, q_raw_to), (k_raw, k_raw_to), (q_rot, q_rot_to), (k_rot, k_rot_to), (v_all, v_to)):
        store(source, target)
    for head in range(4):
        cols = slice(head * 128, head * 128 + 128)
        group = slice(head // 2 * 128, head // 2 * 128 + 128)
        if head % 2 == 0:
            v_turned = v_all[:, group].T
        for i in range(4):
            rows = slice(256 * i, 256 * i + 256)
            q = q_rot[rows, cols]
            total = jnp.zeros((1, 256), f32)
            o = jnp.zeros((HEAD_SIZE, 256), f32)
            for j in range(i + 1):
                keys = slice(256 * j, 256 * j + 256)
                s = dot(k_rot[keys, group], q, NT)
                p = jnp.where(allowed(start[:, rows], i, j), jnp.exp2(s), 0.0)
                total += jnp.sum(p, axis=0, keepdims=True)
                o += dot(v_turned[:, keys], p.astype(bf), NN)
            mixed[rows, cols] = (o / total).T.astype(bf)
            total_log[head, :, rows] = jnp.log2(total)
    for k, part, target in ((2, far, far_to), (1, left, left_to), (3, right, right_to), (0, own, own_to)):
        rows = position_rows(mixed, lax.rem(z + k, 4))
        part[...] = dot(rows, weight_out[...], NT).astype(bf).reshape(2, 128, MODEL_WIDTH)
        store(part, target)
    store(mixed, mixed_to)
    for copy in stores:
        copy.wait()


def forward(info, start, rows, packs, cosine, sine):
    length = cosine.shape[0]
    stored = [
        struct((length, 512)), struct((length, 256)), struct((length, 512)), struct((length, 256)),
        struct((length, 256)), struct((MODEL_WIDTH, 1024)), struct((MODEL_WIDTH, 512)), struct((length, 512)),
    ]
    part = struct((2, 128, MODEL_WIDTH))
    held = [pltpu.VMEM(a.shape, a.dtype) for a in (*packs, cosine, sine)]
    held += [pltpu.VMEM((4, 2, 128, MODEL_WIDTH), bf)]
    held += [pltpu.VMEM(a.shape, a.dtype) for a in stored + [part] * 4]
    return pl.pallas_call(
        forward_kernel,
        out_shape=stored + [part] * 4 + [struct((1, n), f32) for n in (1024, 1024, 128, 128)] + [struct((4, 1, length), f32)],
        in_specs=[SMEM, VMEM] + [HBM] * 8,
        out_specs=[HBM] * 12 + [VMEM] * 5,
        scratch_shapes=held + [pltpu.SemaphoreType.DMA((8 + 12,))],
        compiler_params=params(),
        cost_estimate=COST,
    )(info, start, *rows, *packs, cosine, sine)


def backward_kernel(
    info, start, total_log, gain_q, gain_k,
    gain, m0, m1, m2, m3, weight_out, q_rot, mixed, k_rot, v_in, cosine, sine, q_raw, k_raw, weight, n0, n1, n2, n3,
    parts_to, keep_to, send_to, gain_grad, attn_gain_grad, *scratch,
):
    d_o, d_all, parts, dk_sum, dv_sum, keep, send, out_sems = scratch
    z = info[0]
    for step, chunk in enumerate((m0, m1, m2, m3)):
        rows = chunk[...].reshape(256, MODEL_WIDTH)
        put_rows(d_o, lax.rem(z + 4 - step, 4), dot(rows, weight_out[...], NN).astype(bf))
    q_gain_sum = jnp.zeros((1, HEAD_SIZE), f32)
    k_gain_sum = jnp.zeros((1, HEAD_SIZE), f32)
    for g in range(2):
        group = slice(g * 128, g * 128 + 128)
        k_turned = k_rot[:, group].T
        for head in (2 * g, 2 * g + 1):
            cols = slice(head * 128, head * 128 + 128)
            for i in (3, 2, 1, 0):
                rows = slice(256 * i, 256 * i + 256)
                q = q_rot[rows, cols]
                push = d_o[rows, cols]
                centre = jnp.sum(
                    (push.astype(f32) * mixed[rows, cols].astype(f32)).T, axis=0, keepdims=True
                )
                shift = total_log[head, :, rows]
                grad = jnp.zeros((HEAD_SIZE, 256), f32)
                for j in range(i + 1):
                    keys = slice(256 * j, 256 * j + 256)
                    s = dot(k_rot[keys, group], q, NT)
                    p = jnp.where(allowed(start[:, rows], i, j), jnp.exp2(s - shift), 0.0)
                    d_p = dot(v_in[keys, group], push, NT)
                    d_s = (p * (d_p - centre)).astype(bf)
                    part_k = dot(d_s, q, NN)
                    part_v = dot(p.astype(bf), push, NN)
                    if head % 2 == 0 and i == 3:
                        dk_sum[keys, :] = part_k
                        dv_sum[keys, :] = part_v
                    else:
                        dk_sum[keys, :] += part_k
                        dv_sum[keys, :] += part_v
                    grad += dot(k_turned[:, keys], d_s, NN)
                grad = grad.T * SCORE
                grad = grad * cosine[rows, :] - pltpu.roll(grad, 64, 1) * sine[rows, :]
                scaled, inverse = rms_parts(q_raw[rows, cols].astype(f32))
                q_gain_sum += jnp.sum(grad * scaled, axis=0, keepdims=True)
                d_all[rows, cols] = norm_back(grad, scaled, inverse, gain_q[...]).astype(bf)
        grad = dk_sum[...] * (SCORE / EXPONENT)
        grad = grad * cosine[...] - pltpu.roll(grad, 64, 1) * sine[...]
        scaled, inverse = rms_parts(k_raw[:, group].astype(f32))
        k_gain_sum += jnp.sum(grad * scaled, axis=0, keepdims=True)
        d_all[:, 512 + g * 128 : 640 + g * 128] = norm_back(grad, scaled, inverse, gain_k[...]).astype(bf)
        d_all[:, 768 + g * 128 : 896 + g * 128] = dv_sum[...].astype(bf)
    gain_grad[...] = jnp.concatenate([q_gain_sum, k_gain_sum, jnp.zeros((6, HEAD_SIZE), f32)], axis=0)
    stores = []
    for at in range(4):
        parts[at] = dot(position_rows(d_all, at), weight[...], NT).astype(bf).reshape(2, 128, MODEL_WIDTH)
        stores.append(pltpu.make_async_copy(parts.at[at], parts_to.at[at], out_sems.at[at]))
        stores[-1].start()
    places = [lax.rem(z + 4 - step, 4) for step in range(4)]
    d_rows = [position_rows(d_all, place) for place in places]
    o_rows = [position_rows(mixed, place) for place in places]
    for i in range(4):
        cols = slice(i * 256, i * 256 + 256)
        target = tuple(ref.at[i // 2 * 2 : i // 2 * 2 + 2, i % 2 * 2 : i % 2 * 2 + 2] for ref in (keep, send))
        grad = None
        for right, n in zip(d_rows, (n0, n1, n2, n3)):
            rows = (n[:, :, cols].reshape(256, 256).astype(f32) * gain[:, cols]).astype(bf)
            part = dot(rows, right, TN)
            grad = part if grad is None else grad + part
        put_blocks(grad[:, :512], 0, 2, 256, info[1], *target)
        put_blocks(grad[:, 512:768], 2, 1, 128, info[1], *target)
        put_blocks(grad[:, 768:], 3, 1, 128, info[1], *target)
        attn_gain_grad[cols, :] = jnp.sum(grad * weight[cols, :].astype(f32), axis=1, keepdims=True)
        grad = None
        for right, m in zip(o_rows, (m0, m1, m2, m3)):
            part = dot(m[:, :, cols].reshape(256, 256), right, TN)
            grad = part if grad is None else grad + part
        put_blocks(grad, 4, 2, 256, info[1], *target)
    for source, to in ((keep, keep_to), (send, send_to)):
        stores.append(pltpu.make_async_copy(source, to, out_sems.at[len(stores)]))
        stores[-1].start()
    for copy in stores:
        copy.wait()


def backward(info, small, inputs):
    length = inputs[5].shape[0]
    n = len(inputs)

    def kernel(info, *refs):
        head, sources = refs[: len(small)], refs[len(small) : len(small) + n]
        outs = refs[len(small) + n : len(small) + n + 5]
        buffers = refs[len(small) + n + 5 : len(small) + 2 * n + 5]
        sems, scratch = refs[len(small) + 2 * n + 5], refs[len(small) + 2 * n + 6 :]
        staged = [Staged(a, b, sems.at[k]) for k, (a, b) in enumerate(zip(sources, buffers))]
        backward_kernel(info, *head, *staged, *outs, *scratch)

    parts, grads = struct((4, 2, 128, MODEL_WIDTH)), struct((4, 4, GAIN_AT, 128))
    return pl.pallas_call(
        kernel,
        out_shape=[parts, grads, grads, struct((8, 128), f32), struct((MODEL_WIDTH, 1), f32)],
        in_specs=[SMEM] + [VMEM] * len(small) + [HBM] * n,
        out_specs=[HBM] * 3 + [VMEM] * 2,
        scratch_shapes=[pltpu.VMEM(a.shape, a.dtype) for a in inputs]
        + [pltpu.SemaphoreType.DMA((n,))]
        + [pltpu.VMEM((length, 512), bf), pltpu.VMEM((length, 1024), bf), pltpu.VMEM(parts.shape, bf)]
        + [pltpu.VMEM((length, 128), f32)] * 2
        + [pltpu.VMEM(grads.shape, bf)] * 2
        + [pltpu.SemaphoreType.DMA((6,))],
        compiler_params=params(),
        cost_estimate=COST,
    )(info, *small, *inputs)


def feed_weights_kernel(info, mine, other, *tiles):
    c, y = info[1], info[3]
    for pack, core in ((mine, c), (other, 1 - c)):
        for n in range(3):
            for block in range(3):
                for xl in range(2):
                    column = xl * 384 + block * 128
                    place_rows(
                        pack, core, y, tiles[3 * n + column // 256], 3 * n + block, lambda _, at=column % 256: at, (xl,)
                    )


def feed_kernel(*refs):
    tiles, rows_ref, push_ref = refs[:9], refs[9], refs[10]
    out, d_rows, hidden_out, d_gate_out, d_up_out = refs[11:]
    rows = rows_ref[...].reshape(256, MODEL_WIDTH)
    push = push_ref[...].reshape(256, MODEL_WIDTH)
    total = jnp.zeros((256, MODEL_WIDTH), f32)
    back = jnp.zeros((256, MODEL_WIDTH), f32)
    for j in range(3):
        cols = slice(j * 256, j * 256 + 256)
        gate_w, up_w, down_w = tiles[j][...], tiles[3 + j][...], tiles[6 + j][...]
        gate = dot(rows, gate_w, NN)
        up = dot(rows, up_w, NN)
        d_hidden = dot(push, down_w, NN)
        sigma = jax.nn.sigmoid(gate)
        swish = gate * sigma
        hidden = (swish * up).astype(bf)
        d_gate = (d_hidden * up * (sigma + swish * (1.0 - sigma))).astype(bf)
        d_up = (d_hidden * swish).astype(bf)
        hidden_out[:, cols] = hidden
        d_gate_out[:, cols] = d_gate
        d_up_out[:, cols] = d_up
        total += dot(hidden, down_w, NT)
        back += dot(d_gate, gate_w, NT) + dot(d_up, up_w, NT)
    out[...] = total.astype(bf).reshape(2, 128, MODEL_WIDTH)
    d_rows[...] = back.astype(bf).reshape(2, 128, MODEL_WIDTH)


def feed_chunk(rows, push, weights):
    shapes = [struct((2, 128, MODEL_WIDTH))] * 2 + [struct((256, 768))] * 3
    return staged_call(feed_kernel, shapes, rows, push, resident=weights, limit=FEED_LIMIT)


def put_cores(grad, base, count, per, out):
    for core in range(2):
        for yy in range(2):
            block = grad[yy * 128 + core * 64 : yy * 128 + core * 64 + 64].astype(bf)
            for xl in range(2):
                for j in range(count):
                    at = slice((base + j) * 64, (base + j) * 64 + 64)
                    out[core, xl, yy, at, :] = block[:, xl * per + j * 128 : xl * per + j * 128 + 128]


def put_blocks(grad, base, count, per, core, keep, send):
    for yy in range(2):
        low = grad[yy * 128 : yy * 128 + 64].astype(bf)
        high = grad[yy * 128 + 64 : yy * 128 + 128].astype(bf)
        first = core == 0
        mine = jnp.where(first, low, high)
        other = jnp.where(first, high, low)
        for xl in range(2):
            for j in range(count):
                at = slice((base + j) * 64, (base + j) * 64 + 64)
                cols = slice(xl * per + j * 128, xl * per + j * 128 + 128)
                keep[xl, yy, at, :] = mine[:, cols]
                send[xl, yy, at, :] = other[:, cols]


def feed_grad_kernel(*refs):
    rows, push, hidden, d_gate, d_up = refs[:4], refs[4:8], refs[8:12], refs[12:16], refs[16:20]
    for number, (lefts, rights) in enumerate(((rows, d_gate), (rows, d_up), (push, hidden))):
        total = None
        for left, right in zip(lefts, rights):
            part = dot(left[...].reshape(256, 256), right[...], TN)
            total = part if total is None else total + part
        put_cores(total, number * 3, 3, 384, refs[20])


def feed_grads(rows, push, hidden, d_gate, d_up):
    narrow = pl.BlockSpec((2, 128, 256), lambda i: (0, 0, i))
    whole = pl.BlockSpec((256, 768), lambda i: (0, 0))
    return pl.pallas_call(
        feed_grad_kernel,
        grid=(4,),
        out_shape=struct((2, 4, 4, FEED_ROWS, 128)),
        in_specs=[narrow] * 8 + [whole] * 12,
        out_specs=pl.BlockSpec((2, 2, 2, FEED_ROWS, 128), lambda i: (0, i // 2, i % 2, 0, 0)),
        compiler_params=params(),
        cost_estimate=COST,
    )(*rows, *push, *hidden, *d_gate, *d_up)


def middle_kernel(p0, p1, p2, p3, base, gain, middle, sent):
    total = base[...].astype(f32)
    for part in (p0, p1, p2, p3):
        total += part[...].astype(f32)
    middle[...] = total
    sent[...] = (rms_parts(total)[0] * gain[...]).astype(bf)


def middle_rows(parts, base, gain):
    return staged_call(middle_kernel, [struct(base.shape, f32), struct(base.shape)], *parts, base, gain)


def middle_back_kernel(p0, p1, p2, p3, middle, push, gain, grad_out, sent, gain_grad):
    grad = p0[...].astype(f32)
    for part in (p1, p2, p3):
        grad += part[...].astype(f32)
    scaled, inverse = rms_parts(middle[...])
    gain_grad[...] = jnp.sum(grad * scaled, axis=(0, 1)).reshape(1, MODEL_WIDTH)
    made = push[...].astype(f32) + norm_back(grad, scaled, inverse, gain[...])
    grad_out[...] = made
    sent[...] = made.astype(bf)


def middle_back(parts, middle, push, gain):
    shapes = [struct(middle.shape, f32), struct(middle.shape), struct((1, MODEL_WIDTH), f32)]
    return staged_call(middle_back_kernel, shapes, *parts, middle, push, gain)


def input_back_kernel(info, part, base, middle_grad, gain, keep, sent):
    xl = info[4]
    for place, target in ((xl, keep), (1 - xl, sent)):
        scaled, inverse = rms_parts(base[place].astype(f32))
        grad = norm_back(part[place].astype(f32), scaled, inverse, gain[...])
        target[...] = (middle_grad[place] + grad).astype(target.dtype)


def input_back(info, part, base, middle_grad, gain):
    shapes = [struct(base.shape[1:], f32), struct(base.shape[1:])]
    return staged_call(input_back_kernel, shapes, part, base, middle_grad, gain, info=info)


def pack_kernel(count, *refs):
    sources, pack, held, sems = refs[:count], refs[count], refs[count + 1 : -1], refs[-1]
    copies = [pltpu.make_async_copy(a, b, sems.at[n]) for n, (a, b) in enumerate(zip(sources, held))]
    for copy in copies:
        copy.start()
    at = 0
    for copy, block in zip(copies, held):
        copy.wait()
        rows = block.shape[0]
        for j in range(0, block.shape[1], 128):
            pack[at : at + rows, :] = block[:, j : j + 128].astype(bf)
            at += rows


def pack_weights(sources):
    return pl.pallas_call(
        functools.partial(pack_kernel, len(sources)),
        out_shape=struct((sum(a.size for a in sources) // 128, 128)),
        in_specs=[pl.BlockSpec(memory_space=pl.ANY)] * len(sources),
        out_specs=VMEM,
        scratch_shapes=[pltpu.VMEM(a.shape, a.dtype) for a in sources] + [pltpu.SemaphoreType.DMA((len(sources),))],
        compiler_params=params(),
        cost_estimate=COST,
    )(*sources)


def split_kernel(at, info, *refs):
    sources, outs = refs[:-4], refs[-4:]
    for k in range(4):
        place = lax.rem(info[at] + k, 4)
        total = sources[0][place].astype(f32)
        for source in sources[1:]:
            total += source[place].astype(f32)
        outs[k][...] = total.astype(bf)


def split(info, at, *sources):
    return staged_call(functools.partial(split_kernel, at), [struct(sources[0].shape[1:])] * 4, *sources, info=info)


def adam_kernel(rates, n_parts, *refs):
    grads, refs = refs[:n_parts], refs[n_parts:]
    states, outs = refs[: 3 * len(rates)], refs[3 * len(rates) :]
    at = 0
    for n, rate in enumerate(rates):
        for j in range(0, states[3 * n].shape[1], 128):
            grad = grads[0][at : at + 64, :].astype(f32)
            for other in grads[1:]:
                grad += other[at : at + 64, :].astype(f32)
            cols = slice(j, j + 128)
            made = adamw(*[ref[:, cols] for ref in states[3 * n : 3 * n + 3]], grad, rate)
            for ref, value in zip(outs[3 * n : 3 * n + 3], made):
                ref[:, cols] = value
            at += 64


def adam(parts, states, rates):
    shapes = [struct(a.shape, f32) for a in states]
    return staged_call(functools.partial(adam_kernel, rates, len(parts)), shapes, *parts, *states)


def per_device(
    inputs,
    segments,
    cotangent,
    query_weight,
    query_first,
    query_second,
    key_weight,
    key_first,
    key_second,
    value_weight,
    value_first,
    value_second,
    out_weight,
    out_first,
    out_second,
    gate_weight,
    gate_first,
    gate_second,
    up_weight,
    up_first,
    up_second,
    down_weight,
    down_first,
    down_second,
    gains,
    gain_first,
    gain_second,
):
    width = inputs.shape[2]
    length = segments.shape[1]
    xl, z, y, c = (lax.axis_index(name) for name in ("xl", "z", "y", "c"))
    x = lax.axis_index(X)
    info = jnp.stack([z, c, x, y, xl]).astype(jnp.int32)
    place = (x // 2 * 4 + y) * 2 + c

    gain_slots = lax.dynamic_update_slice(jnp.zeros((32 * 128,), bf), gains.astype(bf), (place * 144,))
    attn_pack = pack_weights((query_weight, key_weight, value_weight, out_weight.T, gain_slots.reshape(32, 128)))
    base = by_sequence(after(inputs, attn_pack), xl)
    push = by_sequence(cotangent, xl)
    feed_pack = pack_weights((gate_weight, up_weight, down_weight.T))
    segment = lax.dynamic_index_in_dim(segments, xl, 0, keepdims=False)
    attn_packs = after(fetch(attn_pack, "y"), base)

    attn_rows = lax.all_gather(jnp.stack(attn_packs), X)
    sent_one = rms_parts(base.astype(f32))[0].astype(bf)
    rows_one = fetch(sent_one, "z")
    cosine, sine, start = rope_tables(after(segment, sent_one), HEAD_SIZE)
    feed_packs = fetch(after(feed_pack, cosine, sent_one, push), "y")
    attn_rows, rows_one, feed_packs, cosine, sine, start = lax.optimization_barrier(
        (attn_rows, rows_one, feed_packs, cosine, sine, start)
    )
    attn_other = swap(attn_rows, "c")
    push_all = fetch(after(push, rows_one), "z")
    feed_rows = lax.all_gather(jnp.stack(feed_packs), X)

    made = forward(info, start, rows_one, (attn_rows, attn_other), cosine, sine)
    q_raw, k_raw, q_rot, k_rot, value, w_qkv, w_out, mixed, far, left, right, own = made[:12]
    attn_gain, feed_gain, query_gain, key_gain, total_log = made[12:]
    out_parts, push_all = lax.optimization_barrier(((own, left, far, right), push_all))
    out_parts = spread(out_parts, "z")
    middle, sent_two = middle_rows(out_parts, base, feed_gain)
    feed_rows = after(feed_rows, sent_two)
    feed_other = swap(feed_rows, "c")
    feed_weights = pl.pallas_call(
        feed_weights_kernel,
        out_shape=[struct((width, 256))] * 9,
        in_specs=[SMEM, VMEM, VMEM],
        out_specs=[VMEM] * 9,
        compiler_params=params(FEED_LIMIT),
        cost_estimate=COST,
    )(info, feed_rows, feed_other)
    rows_two = fetch(sent_two, "z")
    own = feed_chunk(rows_two[0], push_all[0], feed_weights)
    left = feed_chunk(after(rows_two[1], own), push_all[1], feed_weights)
    right = feed_chunk(after(rows_two[3], left), push_all[3], feed_weights)
    two_left = lax.ppermute(left[1], "z", ring(4, 3))
    far = feed_chunk(after(rows_two[2], right, two_left), push_all[2], feed_weights)
    two_far = lax.ppermute(far[1], "z", ring(4, 2))
    two_right = lax.ppermute(right[1], "z", ring(4, 1))
    outs, _, hiddens, d_gates, d_ups = zip(own, left, far, right)
    feed_grad = feed_grads(rows_two, push_all, hiddens, d_gates, d_ups)
    middle_grad, sent_middle, feed_gain_grad = middle_back(
        [own[1], two_left, two_right, two_far], middle, push, feed_gain
    )
    mixed_rows = fetch(sent_middle, "z")
    feed_sum = lax.psum_scatter(after(feed_grad, sent_middle), "c", scatter_dimension=0, tiled=False)
    mixed_rows, feed_sum = lax.optimization_barrier((mixed_rows, feed_sum))
    feed_sum = lax.psum_scatter(feed_sum, X, scatter_dimension=0, tiled=False)
    outs = after(outs, mixed_rows)
    out_parts = spread([outs[0], outs[3], outs[2], outs[1]], "z")
    one_parts, attn_keep, attn_send, head_gain_grads, attn_gain_grad = backward(
        info,
        (start, total_log, query_gain, key_gain, attn_gain),
        (*mixed_rows, w_out, q_rot, mixed, k_rot, value, cosine, sine, q_raw, k_raw, w_qkv, *rows_one),
    )
    attn_send, one_parts, out_parts = lax.optimization_barrier((attn_send, one_parts, out_parts))
    one_parts = lax.psum_scatter(one_parts, "z", scatter_dimension=0, tiled=False)
    x_parts = split(info, 2, attn_keep, swap(attn_send, "c"))
    feed_sum = lax.psum_scatter(after(feed_sum, x_parts), "y", scatter_dimension=0, tiled=False)
    result = by_sequence((middle + total(after(out_parts, x_parts))).astype(bf), xl)
    x_parts = spread(x_parts, X)
    one_parts = after(one_parts, x_parts[1])
    input_keep, input_sent = input_back(info, one_parts, base, middle_grad, attn_gain)
    attn_gain_grad = (attn_gain_grad.reshape(1, width) / attn_gain)[0]
    gain_grad = jnp.concatenate([attn_gain_grad, feed_gain_grad[0], head_gain_grads[0], head_gain_grads[1]])
    gain_parts = jnp.broadcast_to(gain_grad.reshape(16, 1, 144), (16, 8, 144)).reshape(128, 144)
    gain_sum = jnp.sum(lax.all_to_all(after(gain_parts, x_parts[1]), ALL, 0, 0, tiled=True), axis=0)
    y_parts = split(info, 3, *after(x_parts, result))
    feed_sum = after(feed_sum, y_parts)
    y_parts = spread(y_parts, "y")
    input_other = swap(input_sent, "xl").astype(f32)
    first = xl == 0
    input_grad = jnp.stack([jnp.where(first, input_keep, input_other), jnp.where(first, input_other, input_keep)])

    wide_rate = matrix_rate * MODEL_WIDTH ** (-0.5)
    gate_up_down = adam(
        [feed_sum],
        [gate_weight, gate_first, gate_second, up_weight, up_first, up_second]
        + [down_weight.T, down_first.T, down_second.T],
        (wide_rate, wide_rate, matrix_rate * FF ** (-0.5)),
    )
    attn_new = adam(
        y_parts,
        [query_weight, query_first, query_second, key_weight, key_first, key_second]
        + [value_weight, value_first, value_second, out_weight.T, out_first.T, out_second.T],
        (wide_rate, wide_rate, wide_rate, matrix_rate * WO_FAN ** (-0.5)),
    )
    gains_new = adamw(gains, gain_first, gain_second, gain_sum, gain_rate)
    updates = (*attn_new[:9], *[a.T for a in attn_new[9:]], *gate_up_down[:6], *[a.T for a in gate_up_down[6:]])
    return (result, input_grad, *updates, *gains_new)


def solution(mesh):
    split = Mesh(mesh.devices.reshape(2, 4, 2, 2, 4), ALL)
    rows = P(DP, TENSOR, None)
    wide = (P(DP, TENSOR),) * 3
    tall = (P(TENSOR, DP),) * 3
    flat = (P(DP),) * 3
    weights = wide * 3 + tall + wide * 2 + tall + flat
    return jax.shard_map(
        per_device,
        mesh=split,
        in_specs=(rows, P(DP, None), rows) + weights,
        out_specs=(rows, rows) + weights,
        check_vma=False,
    )
```

```python
import functools
import math

import jax
import jax.numpy as jnp
from jax import lax
from jax.experimental import pallas as pl
from jax.experimental.pallas import tpu as pltpu
from jax.sharding import Mesh
from jax.sharding import PartitionSpec as P

MODEL_WIDTH = 1024
QUERY_HEADS = 16
KEY_VALUE_HEADS = 8
HEAD_SIZE = 128
FF = 3072
STEP = 10
WO_FAN = 40

norm_eps = 1e-06
rope_base = 1000000.0
beta_one = 0.9
beta_two = 0.95
adam_eps = 1e-08
decay_rate = 0.1
matrix_rate = 2.5
gain_rate = 0.5
doc_limit = 3

bf = jnp.bfloat16
f32 = jnp.float32
X = ("xh", "xl")
ALL = ("xh", "y", "c", "xl", "z")
DP = ("xh", "y", "c")
TENSOR = ("xl", "z")


SCORE = HEAD_SIZE ** (-0.5)
EXPONENT = SCORE / math.log(2.0)
VMEM = pl.BlockSpec(memory_space=pltpu.VMEM)
SMEM = pl.BlockSpec(memory_space=pltpu.SMEM)
HBM = pl.BlockSpec(memory_space=pltpu.HBM)
LIMIT = 50 * 1024 * 1024
FEED_LIMIT = 24 * 1024 * 1024
GAIN_AT = 6 * 64
ATTN_ROWS = GAIN_AT + 32
FEED_ROWS = 9 * 64


COST = pl.CostEstimate(flops=1, bytes_accessed=1, transcendentals=0)


def params(limit=LIMIT):
    return pltpu.CompilerParams(vmem_limit_bytes=limit)


class Staged:
    def __init__(self, source, buffer, sem):
        self.buffer, self.copy = buffer, pltpu.make_async_copy(source, buffer, sem)
        self.shape = buffer.shape
        self.copy.start()

    def __getitem__(self, at):
        if self.copy is not None:
            self.copy.wait()
            self.copy = None
        return self.buffer[at]


def staged_kernel(kernel, n_head, n_in, n_out, *refs):
    head, sources = refs[:n_head], refs[n_head : n_head + n_in]
    targets = refs[n_head + n_in : n_head + n_in + n_out]
    buffers = refs[n_head + n_in + n_out : n_head + 2 * n_in + n_out]
    outs, sems = refs[n_head + 2 * n_in + n_out : -1], refs[-1]
    kernel(*head, *[Staged(a, b, sems.at[n]) for n, (a, b) in enumerate(zip(sources, buffers))], *outs)
    stores = [pltpu.make_async_copy(a, b, sems.at[n_in + n]) for n, (a, b) in enumerate(zip(outs, targets))]
    for copy in stores:
        copy.start()
    for copy in stores:
        copy.wait()


def staged_call(kernel, out_shape, *inputs, info=None, resident=(), limit=LIMIT):
    head = () if info is None else (info,)
    n_in, n_out = len(inputs), len(out_shape)
    return pl.pallas_call(
        functools.partial(staged_kernel, kernel, len(head) + len(resident), n_in, n_out),
        out_shape=out_shape,
        in_specs=[SMEM] * len(head) + [VMEM] * len(resident) + [HBM] * n_in,
        out_specs=[HBM] * n_out,
        scratch_shapes=[pltpu.VMEM(a.shape, a.dtype) for a in (*inputs, *out_shape)]
        + [pltpu.SemaphoreType.DMA((n_in + n_out,))],
        compiler_params=params(limit),
        cost_estimate=COST,
    )(*head, *resident, *inputs)


def struct(shape, dtype=bf):
    return jax.ShapeDtypeStruct(shape, dtype)


def dot(left, right, dims):
    return lax.dot_general(left, right, (dims, ((), ())), preferred_element_type=f32)


NN = ((1,), (0,))
NT = ((1,), (1,))
TN = ((0,), (0,))


def rms_parts(rows):
    inverse = lax.rsqrt(jnp.mean(rows * rows, axis=-1, keepdims=True) + norm_eps)
    return (rows * inverse, inverse)


def norm_back(grad, scaled, inverse, gain):
    pushed = grad * gain
    return inverse * (pushed - scaled * jnp.mean(pushed * scaled, axis=-1, keepdims=True))


def positions(segment):
    before = jnp.zeros(segment.shape, jnp.int32)
    for level in range(doc_limit):
        count = jnp.sum((segment == level).astype(jnp.int32), axis=-1, keepdims=True)
        before = before + jnp.where(segment > level, count, 0)
    return lax.broadcasted_iota(jnp.int32, segment.shape, segment.ndim - 1) - before


def rope_tables(segment, width):
    place = positions(segment)
    start = jnp.arange(segment.shape[0], dtype=jnp.int32) - place
    place = place.astype(f32)
    index = jnp.arange(width // 2, dtype=f32)
    inverse = jnp.exp(index * (-2.0 * math.log(rope_base) / width))
    angle = place[..., None] * inverse
    cosine = jnp.cos(angle)
    sine = jnp.sin(angle)
    cosine = jnp.concatenate([cosine, cosine], axis=-1)
    sine = jnp.concatenate([-sine, sine], axis=-1)
    return cosine, sine, start[None, :]


def ring(count, step):
    return [(i, (i + step) % count) for i in range(count)]


def swap(value, axis):
    return lax.ppermute(value, axis, ring(2, 1))


def fetch(value, axis):
    far = lax.ppermute(value, axis, ring(4, 2))
    left = lax.ppermute(value, axis, ring(4, 1))
    right = lax.ppermute(value, axis, ring(4, 3))
    return [value, left, far, right]


def spread(parts, axis):
    far = lax.ppermute(parts[2], axis, ring(4, 2))
    left = lax.ppermute(parts[1], axis, ring(4, 1))
    right = lax.ppermute(parts[3], axis, ring(4, 3))
    return [parts[0], left, far, right]


def total(parts):
    return sum(part.astype(f32) for part in parts)


def after(value, *others):
    return lax.optimization_barrier((value, others))[0]


def by_sequence(value, xl):
    keep = lax.dynamic_index_in_dim(value, xl, 0, keepdims=False)
    other = swap(lax.dynamic_index_in_dim(value, 1 - xl, 0, keepdims=False), "xl")
    first = xl == 0
    return jnp.stack([jnp.where(first, keep, other), jnp.where(first, other, keep)])


def adamw(weight, first, second, grad, rate):
    first_new = beta_one * first + (1.0 - beta_one) * grad
    second_new = beta_two * second + (1.0 - beta_two) * grad * grad
    ratio = (
        first_new
        / (1.0 - beta_one**STEP)
        / (jnp.sqrt(second_new / (1.0 - beta_two**STEP)) + adam_eps)
    )
    return (weight - rate * (ratio + decay_rate * weight), first_new, second_new)


def place_rows(pack, core, y, target, block, column, halves=(0, 1)):
    for xh in range(2):
        for j in range(4):
            at = pl.multiple_of((xh * 4 + lax.rem(y + 4 - j, 4)) * 128 + core * 64, 64)
            for xl in halves:
                target[pl.ds(at, 64), column(xl) : column(xl) + 128] = pack[
                    xh * 2 + xl, j, block * 64 : block * 64 + 64, :
                ]


def allowed(start_row, i, j):
    key = lax.broadcasted_iota(jnp.int32, (256, 256), 0) + 256 * j
    seen = key >= start_row
    if i == j:
        seen = seen & (key <= lax.broadcasted_iota(jnp.int32, (256, 256), 1) + 256 * i)
    return seen


def position_rows(ref, at, cols=slice(None)):
    low = pl.multiple_of(at * 128, 128)
    return jnp.concatenate([ref[pl.ds(low, 128), cols], ref[pl.ds(low + 512, 128), cols]], axis=0)


def put_rows(ref, at, value, cols=slice(None)):
    low = pl.multiple_of(at * 128, 128)
    ref[pl.ds(low, 128), cols] = value[:128]
    ref[pl.ds(low + 512, 128), cols] = value[128:]


def forward_kernel(
    info, start, n0, n1, n2, n3, mine_in, other_in, cos_in, sin_in,
    q_raw_to, k_raw_to, q_rot_to, k_rot_to, v_to, weight_to, weight_out_to, mixed_to,
    far_to, left_to, right_to, own_to, gain_one, gain_two, gain_q, gain_k, total_log,
    mine, other, cosine, sine, rows_in, q_raw, k_raw, q_rot, k_rot, v_all, weight, weight_out, mixed,
    far, left, right, own, sems,
):
    z, c, y = info[0], info[1], info[3]
    pairs = [(mine_in, mine), (other_in, other), (cos_in, cosine), (sin_in, sine)]
    pairs += [(chunk, rows_in.at[n]) for n, chunk in enumerate((n0, n1, n2, n3))]
    copies = [pltpu.make_async_copy(a, b, sems.at[n]) for n, (a, b) in enumerate(pairs)]
    for copy in copies:
        copy.start()
    stores = []

    def store(source, target):
        copy = pltpu.make_async_copy(source, target, sems.at[8 + len(stores)])
        copy.start()
        stores.append(copy)

    gain = jnp.zeros((32, 128), f32)
    for copy, pack, core in ((copies[0], mine, c), (copies[1], other, 1 - c)):
        copy.wait()
        place_rows(pack, core, y, weight, 0, lambda xl: xl * 256)
        place_rows(pack, core, y, weight, 1, lambda xl: xl * 256 + 128)
        place_rows(pack, core, y, weight, 2, lambda xl: xl * 128 + 512)
        place_rows(pack, core, y, weight, 3, lambda xl: xl * 128 + 768)
        place_rows(pack, core, y, weight_out, 4, lambda xl: xl * 256)
        place_rows(pack, core, y, weight_out, 5, lambda xl: xl * 256 + 128)
        for i in range(4):
            for j in range(4):
                gain += pack[i, j, GAIN_AT:ATTN_ROWS, :].astype(f32)
    gain = gain * 0.5
    for j in range(8):
        gain_one[:, j * 128 : j * 128 + 128] = gain[j : j + 1, :]
        gain_two[:, j * 128 : j * 128 + 128] = gain[8 + j : 9 + j, :]
    gain_q[...] = gain[16:17, :]
    gain_k[...] = gain[17:18, :]
    store(weight, weight_to)
    store(weight_out, weight_out_to)
    copies[2].wait()
    copies[3].wait()
    for step in range(4):
        copies[4 + step].wait()
        at = lax.rem(z + 4 - step, 4)
        rows = rows_in[step].reshape(256, MODEL_WIDTH)
        rows = jnp.concatenate(
            [
                (rows[:, j * 128 : j * 128 + 128].astype(f32) * gain[j : j + 1, :]).astype(bf)
                for j in range(8)
            ],
            axis=1,
        )
        made = dot(rows, weight[...], NN)
        cos, sin = position_rows(cosine, at), position_rows(sine, at)
        put_rows(q_raw, at, made[:, :512].astype(bf))
        put_rows(k_raw, at, made[:, 512:768].astype(bf))
        put_rows(v_all, at, made[:, 768:].astype(bf))
        for head in range(6):
            cols = slice(head * 128, head * 128 + 128)
            scaled, _ = rms_parts(made[:, cols])
            scaled = scaled * (gain[16:17, :] if head < 4 else gain[17:18, :])
            turned = scaled * cos + pltpu.roll(scaled, 64, 1) * sin
            if head < 4:
                put_rows(q_rot, at, (turned * EXPONENT).astype(bf), cols)
            else:
                put_rows(k_rot, at, turned.astype(bf), slice(head * 128 - 512, head * 128 - 384))
    for source, target in ((q_raw, q_raw_to), (k_raw, k_raw_to), (q_rot, q_rot_to), (k_rot, k_rot_to), (v_all, v_to)):
        store(source, target)
    for head in range(4):
        cols = slice(head * 128, head * 128 + 128)
        group = slice(head // 2 * 128, head // 2 * 128 + 128)
        if head % 2 == 0:
            v_turned = v_all[:, group].T
        for i in range(4):
            rows = slice(256 * i, 256 * i + 256)
            q = q_rot[rows, cols]
            total = jnp.zeros((1, 256), f32)
            o = jnp.zeros((HEAD_SIZE, 256), f32)
            for j in range(i + 1):
                keys = slice(256 * j, 256 * j + 256)
                s = dot(k_rot[keys, group], q, NT)
                p = jnp.where(allowed(start[:, rows], i, j), jnp.exp2(s), 0.0)
                total += jnp.sum(p, axis=0, keepdims=True)
                o += dot(v_turned[:, keys], p.astype(bf), NN)
            mixed[rows, cols] = (o / total).T.astype(bf)
            total_log[head, :, rows] = jnp.log2(total)
    for k, part, target in ((2, far, far_to), (1, left, left_to), (3, right, right_to), (0, own, own_to)):
        rows = position_rows(mixed, lax.rem(z + k, 4))
        part[...] = dot(rows, weight_out[...], NT).astype(bf).reshape(2, 128, MODEL_WIDTH)
        store(part, target)
    store(mixed, mixed_to)
    for copy in stores:
        copy.wait()


def forward(info, start, rows, packs, cosine, sine):
    length = cosine.shape[0]
    stored = [
        struct((length, 512)), struct((length, 256)), struct((length, 512)), struct((length, 256)),
        struct((length, 256)), struct((MODEL_WIDTH, 1024)), struct((MODEL_WIDTH, 512)), struct((length, 512)),
    ]
    part = struct((2, 128, MODEL_WIDTH))
    held = [pltpu.VMEM(a.shape, a.dtype) for a in (*packs, cosine, sine)]
    held += [pltpu.VMEM((4, 2, 128, MODEL_WIDTH), bf)]
    held += [pltpu.VMEM(a.shape, a.dtype) for a in stored + [part] * 4]
    return pl.pallas_call(
        forward_kernel,
        out_shape=stored + [part] * 4 + [struct((1, n), f32) for n in (1024, 1024, 128, 128)] + [struct((4, 1, length), f32)],
        in_specs=[SMEM, VMEM] + [HBM] * 8,
        out_specs=[HBM] * 12 + [VMEM] * 5,
        scratch_shapes=held + [pltpu.SemaphoreType.DMA((8 + 12,))],
        compiler_params=params(),
        cost_estimate=COST,
    )(info, start, *rows, *packs, cosine, sine)


def backward_kernel(
    info, start, total_log, gain_q, gain_k,
    gain, m0, m1, m2, m3, weight_out, q_rot, mixed, k_rot, v_in, cosine, sine, q_raw, k_raw, weight, n0, n1, n2, n3,
    parts_to, keep_to, send_to, gain_grad, attn_gain_grad, *scratch,
):
    d_o, d_all, parts, dk_sum, dv_sum, keep, send, out_sems = scratch
    z = info[0]
    for step, chunk in enumerate((m0, m1, m2, m3)):
        rows = chunk[...].reshape(256, MODEL_WIDTH)
        put_rows(d_o, lax.rem(z + 4 - step, 4), dot(rows, weight_out[...], NN).astype(bf))
    q_gain_sum = jnp.zeros((1, HEAD_SIZE), f32)
    k_gain_sum = jnp.zeros((1, HEAD_SIZE), f32)
    for g in range(2):
        group = slice(g * 128, g * 128 + 128)
        k_turned = k_rot[:, group].T
        for head in (2 * g, 2 * g + 1):
            cols = slice(head * 128, head * 128 + 128)
            for i in (3, 2, 1, 0):
                rows = slice(256 * i, 256 * i + 256)
                q = q_rot[rows, cols]
                push = d_o[rows, cols]
                centre = jnp.sum(
                    (push.astype(f32) * mixed[rows, cols].astype(f32)).T, axis=0, keepdims=True
                )
                shift = total_log[head, :, rows]
                grad = jnp.zeros((HEAD_SIZE, 256), f32)
                for j in range(i + 1):
                    keys = slice(256 * j, 256 * j + 256)
                    s = dot(k_rot[keys, group], q, NT)
                    p = jnp.where(allowed(start[:, rows], i, j), jnp.exp2(s - shift), 0.0)
                    d_p = dot(v_in[keys, group], push, NT)
                    d_s = (p * (d_p - centre)).astype(bf)
                    part_k = dot(d_s, q, NN)
                    part_v = dot(p.astype(bf), push, NN)
                    if head % 2 == 0 and i == 3:
                        dk_sum[keys, :] = part_k
                        dv_sum[keys, :] = part_v
                    else:
                        dk_sum[keys, :] += part_k
                        dv_sum[keys, :] += part_v
                    grad += dot(k_turned[:, keys], d_s, NN)
                grad = grad.T * SCORE
                grad = grad * cosine[rows, :] - pltpu.roll(grad, 64, 1) * sine[rows, :]
                scaled, inverse = rms_parts(q_raw[rows, cols].astype(f32))
                q_gain_sum += jnp.sum(grad * scaled, axis=0, keepdims=True)
                d_all[rows, cols] = norm_back(grad, scaled, inverse, gain_q[...]).astype(bf)
        grad = dk_sum[...] * (SCORE / EXPONENT)
        grad = grad * cosine[...] - pltpu.roll(grad, 64, 1) * sine[...]
        scaled, inverse = rms_parts(k_raw[:, group].astype(f32))
        k_gain_sum += jnp.sum(grad * scaled, axis=0, keepdims=True)
        d_all[:, 512 + g * 128 : 640 + g * 128] = norm_back(grad, scaled, inverse, gain_k[...]).astype(bf)
        d_all[:, 768 + g * 128 : 896 + g * 128] = dv_sum[...].astype(bf)
    gain_grad[...] = jnp.concatenate([q_gain_sum, k_gain_sum, jnp.zeros((6, HEAD_SIZE), f32)], axis=0)
    stores = []
    for at in range(4):
        parts[at] = dot(position_rows(d_all, at), weight[...], NT).astype(bf).reshape(2, 128, MODEL_WIDTH)
        stores.append(pltpu.make_async_copy(parts.at[at], parts_to.at[at], out_sems.at[at]))
        stores[-1].start()
    places = [lax.rem(z + 4 - step, 4) for step in range(4)]
    d_rows = [position_rows(d_all, place) for place in places]
    o_rows = [position_rows(mixed, place) for place in places]
    for i in range(4):
        cols = slice(i * 256, i * 256 + 256)
        target = tuple(ref.at[i // 2 * 2 : i // 2 * 2 + 2, i % 2 * 2 : i % 2 * 2 + 2] for ref in (keep, send))
        grad = None
        for right, n in zip(d_rows, (n0, n1, n2, n3)):
            rows = (n[:, :, cols].reshape(256, 256).astype(f32) * gain[:, cols]).astype(bf)
            part = dot(rows, right, TN)
            grad = part if grad is None else grad + part
        put_blocks(grad[:, :512], 0, 2, 256, info[1], *target)
        put_blocks(grad[:, 512:768], 2, 1, 128, info[1], *target)
        put_blocks(grad[:, 768:], 3, 1, 128, info[1], *target)
        attn_gain_grad[cols, :] = jnp.sum(grad * weight[cols, :].astype(f32), axis=1, keepdims=True)
        grad = None
        for right, m in zip(o_rows, (m0, m1, m2, m3)):
            part = dot(m[:, :, cols].reshape(256, 256), right, TN)
            grad = part if grad is None else grad + part
        put_blocks(grad, 4, 2, 256, info[1], *target)
    for source, to in ((keep, keep_to), (send, send_to)):
        stores.append(pltpu.make_async_copy(source, to, out_sems.at[len(stores)]))
        stores[-1].start()
    for copy in stores:
        copy.wait()


def backward(info, small, inputs):
    length = inputs[5].shape[0]
    n = len(inputs)

    def kernel(info, *refs):
        head, sources = refs[: len(small)], refs[len(small) : len(small) + n]
        outs = refs[len(small) + n : len(small) + n + 5]
        buffers = refs[len(small) + n + 5 : len(small) + 2 * n + 5]
        sems, scratch = refs[len(small) + 2 * n + 5], refs[len(small) + 2 * n + 6 :]
        staged = [Staged(a, b, sems.at[k]) for k, (a, b) in enumerate(zip(sources, buffers))]
        backward_kernel(info, *head, *staged, *outs, *scratch)

    parts, grads = struct((4, 2, 128, MODEL_WIDTH)), struct((4, 4, GAIN_AT, 128))
    return pl.pallas_call(
        kernel,
        out_shape=[parts, grads, grads, struct((8, 128), f32), struct((MODEL_WIDTH, 1), f32)],
        in_specs=[SMEM] + [VMEM] * len(small) + [HBM] * n,
        out_specs=[HBM] * 3 + [VMEM] * 2,
        scratch_shapes=[pltpu.VMEM(a.shape, a.dtype) for a in inputs]
        + [pltpu.SemaphoreType.DMA((n,))]
        + [pltpu.VMEM((length, 512), bf), pltpu.VMEM((length, 1024), bf), pltpu.VMEM(parts.shape, bf)]
        + [pltpu.VMEM((length, 128), f32)] * 2
        + [pltpu.VMEM(grads.shape, bf)] * 2
        + [pltpu.SemaphoreType.DMA((6,))],
        compiler_params=params(),
        cost_estimate=COST,
    )(info, *small, *inputs)


def feed_weights_kernel(info, mine, other, *tiles):
    c, y = info[1], info[3]
    for pack, core in ((mine, c), (other, 1 - c)):
        for n in range(3):
            for block in range(3):
                for xl in range(2):
                    column = xl * 384 + block * 128
                    place_rows(
                        pack, core, y, tiles[3 * n + column // 256], 3 * n + block, lambda _, at=column % 256: at, (xl,)
                    )


def feed_kernel(*refs):
    tiles, rows_ref, push_ref = refs[:9], refs[9], refs[10]
    out, d_rows, hidden_out, d_gate_out, d_up_out = refs[11:]
    rows = rows_ref[...].reshape(256, MODEL_WIDTH)
    push = push_ref[...].reshape(256, MODEL_WIDTH)
    total = jnp.zeros((256, MODEL_WIDTH), f32)
    back = jnp.zeros((256, MODEL_WIDTH), f32)
    for j in range(3):
        cols = slice(j * 256, j * 256 + 256)
        gate_w, up_w, down_w = tiles[j][...], tiles[3 + j][...], tiles[6 + j][...]
        gate = dot(rows, gate_w, NN)
        up = dot(rows, up_w, NN)
        d_hidden = dot(push, down_w, NN)
        sigma = jax.nn.sigmoid(gate)
        swish = gate * sigma
        hidden = (swish * up).astype(bf)
        d_gate = (d_hidden * up * (sigma + swish * (1.0 - sigma))).astype(bf)
        d_up = (d_hidden * swish).astype(bf)
        hidden_out[:, cols] = hidden
        d_gate_out[:, cols] = d_gate
        d_up_out[:, cols] = d_up
        total += dot(hidden, down_w, NT)
        back += dot(d_gate, gate_w, NT) + dot(d_up, up_w, NT)
    out[...] = total.astype(bf).reshape(2, 128, MODEL_WIDTH)
    d_rows[...] = back.astype(bf).reshape(2, 128, MODEL_WIDTH)


def feed_chunk(rows, push, weights):
    shapes = [struct((2, 128, MODEL_WIDTH))] * 2 + [struct((256, 768))] * 3
    return staged_call(feed_kernel, shapes, rows, push, resident=weights, limit=FEED_LIMIT)


def put_cores(grad, base, count, per, out):
    for core in range(2):
        for yy in range(2):
            block = grad[yy * 128 + core * 64 : yy * 128 + core * 64 + 64].astype(bf)
            for xl in range(2):
                for j in range(count):
                    at = slice((base + j) * 64, (base + j) * 64 + 64)
                    out[core, xl, yy, at, :] = block[:, xl * per + j * 128 : xl * per + j * 128 + 128]


def put_blocks(grad, base, count, per, core, keep, send):
    for yy in range(2):
        low = grad[yy * 128 : yy * 128 + 64].astype(bf)
        high = grad[yy * 128 + 64 : yy * 128 + 128].astype(bf)
        first = core == 0
        mine = jnp.where(first, low, high)
        other = jnp.where(first, high, low)
        for xl in range(2):
            for j in range(count):
                at = slice((base + j) * 64, (base + j) * 64 + 64)
                cols = slice(xl * per + j * 128, xl * per + j * 128 + 128)
                keep[xl, yy, at, :] = mine[:, cols]
                send[xl, yy, at, :] = other[:, cols]


def feed_grad_kernel(*refs):
    rows, push, hidden, d_gate, d_up = refs[:4], refs[4:8], refs[8:12], refs[12:16], refs[16:20]
    for number, (lefts, rights) in enumerate(((rows, d_gate), (rows, d_up), (push, hidden))):
        total = None
        for left, right in zip(lefts, rights):
            part = dot(left[...].reshape(256, 256), right[...], TN)
            total = part if total is None else total + part
        put_cores(total, number * 3, 3, 384, refs[20])


def feed_grads(rows, push, hidden, d_gate, d_up):
    narrow = pl.BlockSpec((2, 128, 256), lambda i: (0, 0, i))
    whole = pl.BlockSpec((256, 768), lambda i: (0, 0))
    return pl.pallas_call(
        feed_grad_kernel,
        grid=(4,),
        out_shape=struct((2, 4, 4, FEED_ROWS, 128)),
        in_specs=[narrow] * 8 + [whole] * 12,
        out_specs=pl.BlockSpec((2, 2, 2, FEED_ROWS, 128), lambda i: (0, i // 2, i % 2, 0, 0)),
        compiler_params=params(),
        cost_estimate=COST,
    )(*rows, *push, *hidden, *d_gate, *d_up)


def middle_kernel(p0, p1, p2, p3, base, gain, middle, sent):
    total = base[...].astype(f32)
    for part in (p0, p1, p2, p3):
        total += part[...].astype(f32)
    middle[...] = total
    sent[...] = (rms_parts(total)[0] * gain[...]).astype(bf)


def middle_rows(parts, base, gain):
    return staged_call(middle_kernel, [struct(base.shape, f32), struct(base.shape)], *parts, base, gain)


def middle_back_kernel(p0, p1, p2, p3, middle, push, gain, grad_out, sent, gain_grad):
    grad = p0[...].astype(f32)
    for part in (p1, p2, p3):
        grad += part[...].astype(f32)
    scaled, inverse = rms_parts(middle[...])
    gain_grad[...] = jnp.sum(grad * scaled, axis=(0, 1)).reshape(1, MODEL_WIDTH)
    made = push[...].astype(f32) + norm_back(grad, scaled, inverse, gain[...])
    grad_out[...] = made
    sent[...] = made.astype(bf)


def middle_back(parts, middle, push, gain):
    shapes = [struct(middle.shape, f32), struct(middle.shape), struct((1, MODEL_WIDTH), f32)]
    return staged_call(middle_back_kernel, shapes, *parts, middle, push, gain)


def input_back_kernel(info, part, base, middle_grad, gain, keep, sent):
    xl = info[4]
    for place, target in ((xl, keep), (1 - xl, sent)):
        scaled, inverse = rms_parts(base[place].astype(f32))
        grad = norm_back(part[place].astype(f32), scaled, inverse, gain[...])
        target[...] = (middle_grad[place] + grad).astype(target.dtype)


def input_back(info, part, base, middle_grad, gain):
    shapes = [struct(base.shape[1:], f32), struct(base.shape[1:])]
    return staged_call(input_back_kernel, shapes, part, base, middle_grad, gain, info=info)


def pack_kernel(count, *refs):
    sources, pack, held, sems = refs[:count], refs[count], refs[count + 1 : -1], refs[-1]
    copies = [pltpu.make_async_copy(a, b, sems.at[n]) for n, (a, b) in enumerate(zip(sources, held))]
    for copy in copies:
        copy.start()
    at = 0
    for copy, block in zip(copies, held):
        copy.wait()
        rows = block.shape[0]
        for j in range(0, block.shape[1], 128):
            pack[at : at + rows, :] = block[:, j : j + 128].astype(bf)
            at += rows


def pack_weights(sources):
    return pl.pallas_call(
        functools.partial(pack_kernel, len(sources)),
        out_shape=struct((sum(a.size for a in sources) // 128, 128)),
        in_specs=[pl.BlockSpec(memory_space=pl.ANY)] * len(sources),
        out_specs=VMEM,
        scratch_shapes=[pltpu.VMEM(a.shape, a.dtype) for a in sources] + [pltpu.SemaphoreType.DMA((len(sources),))],
        compiler_params=params(),
        cost_estimate=COST,
    )(*sources)


def split_kernel(at, info, *refs):
    sources, outs = refs[:-4], refs[-4:]
    for k in range(4):
        place = lax.rem(info[at] + k, 4)
        total = sources[0][place].astype(f32)
        for source in sources[1:]:
            total += source[place].astype(f32)
        outs[k][...] = total.astype(bf)


def split(info, at, *sources):
    return staged_call(functools.partial(split_kernel, at), [struct(sources[0].shape[1:])] * 4, *sources, info=info)


def adam_kernel(rates, n_parts, *refs):
    grads, refs = refs[:n_parts], refs[n_parts:]
    states, outs = refs[: 3 * len(rates)], refs[3 * len(rates) :]
    at = 0
    for n, rate in enumerate(rates):
        for j in range(0, states[3 * n].shape[1], 128):
            grad = grads[0][at : at + 64, :].astype(f32)
            for other in grads[1:]:
                grad += other[at : at + 64, :].astype(f32)
            cols = slice(j, j + 128)
            made = adamw(*[ref[:, cols] for ref in states[3 * n : 3 * n + 3]], grad, rate)
            for ref, value in zip(outs[3 * n : 3 * n + 3], made):
                ref[:, cols] = value
            at += 64


def adam(parts, states, rates):
    shapes = [struct(a.shape, f32) for a in states]
    return staged_call(functools.partial(adam_kernel, rates, len(parts)), shapes, *parts, *states)


def per_device(
    inputs,
    segments,
    cotangent,
    query_weight,
    query_first,
    query_second,
    key_weight,
    key_first,
    key_second,
    value_weight,
    value_first,
    value_second,
    out_weight,
    out_first,
    out_second,
    gate_weight,
    gate_first,
    gate_second,
    up_weight,
    up_first,
    up_second,
    down_weight,
    down_first,
    down_second,
    gains,
    gain_first,
    gain_second,
):
    width = inputs.shape[2]
    length = segments.shape[1]
    xl, z, y, c = (lax.axis_index(name) for name in ("xl", "z", "y", "c"))
    x = lax.axis_index(X)
    info = jnp.stack([z, c, x, y, xl]).astype(jnp.int32)
    place = (x // 2 * 4 + y) * 2 + c

    gain_slots = lax.dynamic_update_slice(jnp.zeros((32 * 128,), bf), gains.astype(bf), (place * 144,))
    inputs_keep = lax.dynamic_index_in_dim(inputs, xl, 0, keepdims=False)
    inputs_send = lax.dynamic_index_in_dim(inputs, 1 - xl, 0, keepdims=False)
    gain_slots = after(gain_slots, inputs_send)
    attn_pack = pack_weights((query_weight, key_weight, value_weight, out_weight.T, gain_slots.reshape(32, 128)))
    inputs_other = swap(inputs_send, "xl")
    base = jnp.stack(
        [jnp.where(xl == 0, inputs_keep, inputs_other), jnp.where(xl == 0, inputs_other, inputs_keep)]
    )
    push = by_sequence(cotangent, xl)
    feed_pack = pack_weights((gate_weight, up_weight, down_weight.T))
    segment = lax.dynamic_index_in_dim(segments, xl, 0, keepdims=False)
    attn_packs = after(fetch(attn_pack, "y"), base)

    attn_rows = lax.all_gather(jnp.stack(attn_packs), X)
    sent_one = rms_parts(base.astype(f32))[0].astype(bf)
    rows_one = fetch(sent_one, "z")
    cosine, sine, start = rope_tables(after(segment, sent_one), HEAD_SIZE)
    feed_packs = fetch(after(feed_pack, cosine, sent_one, push), "y")
    attn_rows, rows_one, feed_packs, cosine, sine, start = lax.optimization_barrier(
        (attn_rows, rows_one, feed_packs, cosine, sine, start)
    )
    attn_other = swap(attn_rows, "c")
    push_all = fetch(after(push, rows_one), "z")
    feed_rows = lax.all_gather(jnp.stack(feed_packs), X)

    made = forward(info, start, rows_one, (attn_rows, attn_other), cosine, sine)
    q_raw, k_raw, q_rot, k_rot, value, w_qkv, w_out, mixed, far, left, right, own = made[:12]
    attn_gain, feed_gain, query_gain, key_gain, total_log = made[12:]
    out_parts, push_all = lax.optimization_barrier(((own, left, far, right), push_all))
    out_parts = spread(out_parts, "z")
    middle, sent_two = middle_rows(out_parts, base, feed_gain)
    feed_rows = after(feed_rows, sent_two)
    feed_other = swap(feed_rows, "c")
    feed_weights = pl.pallas_call(
        feed_weights_kernel,
        out_shape=[struct((width, 256))] * 9,
        in_specs=[SMEM, VMEM, VMEM],
        out_specs=[VMEM] * 9,
        compiler_params=params(FEED_LIMIT),
        cost_estimate=COST,
    )(info, feed_rows, feed_other)
    rows_two = fetch(sent_two, "z")
    own = feed_chunk(rows_two[0], push_all[0], feed_weights)
    left = feed_chunk(after(rows_two[1], own), push_all[1], feed_weights)
    right = feed_chunk(after(rows_two[3], left), push_all[3], feed_weights)
    two_left = lax.ppermute(left[1], "z", ring(4, 3))
    far = feed_chunk(after(rows_two[2], right, two_left), push_all[2], feed_weights)
    two_far = lax.ppermute(far[1], "z", ring(4, 2))
    two_right = lax.ppermute(right[1], "z", ring(4, 1))
    outs, _, hiddens, d_gates, d_ups = zip(own, left, far, right)
    feed_grad = feed_grads(rows_two, push_all, hiddens, d_gates, d_ups)
    middle_grad, sent_middle, feed_gain_grad = middle_back(
        [own[1], two_left, two_right, two_far], middle, push, feed_gain
    )
    mixed_rows = fetch(sent_middle, "z")
    feed_sum = lax.psum_scatter(after(feed_grad, sent_middle), "c", scatter_dimension=0, tiled=False)
    mixed_rows, feed_sum = lax.optimization_barrier((mixed_rows, feed_sum))
    feed_sum = lax.psum_scatter(feed_sum, X, scatter_dimension=0, tiled=False)
    outs = after(outs, mixed_rows)
    out_parts = spread([outs[0], outs[3], outs[2], outs[1]], "z")
    one_parts, attn_keep, attn_send, head_gain_grads, attn_gain_grad = backward(
        info,
        (start, total_log, query_gain, key_gain, attn_gain),
        (*mixed_rows, w_out, q_rot, mixed, k_rot, value, cosine, sine, q_raw, k_raw, w_qkv, *rows_one),
    )
    attn_send, one_parts, out_parts = lax.optimization_barrier((attn_send, one_parts, out_parts))
    one_parts = lax.psum_scatter(one_parts, "z", scatter_dimension=0, tiled=False)
    x_parts = split(info, 2, attn_keep, swap(attn_send, "c"))
    feed_sum = lax.psum_scatter(after(feed_sum, x_parts), "y", scatter_dimension=0, tiled=False)
    result = by_sequence((middle + total(after(out_parts, x_parts))).astype(bf), xl)
    x_parts = spread(x_parts, X)
    one_parts = after(one_parts, x_parts[1])
    input_keep, input_sent = input_back(info, one_parts, base, middle_grad, attn_gain)
    attn_gain_grad = (attn_gain_grad.reshape(1, width) / attn_gain)[0]
    gain_grad = jnp.concatenate([attn_gain_grad, feed_gain_grad[0], head_gain_grads[0], head_gain_grads[1]])
    gain_parts = jnp.broadcast_to(gain_grad.reshape(16, 1, 144), (16, 8, 144)).reshape(128, 144)
    gain_sum = jnp.sum(lax.all_to_all(after(gain_parts, x_parts[1]), ALL, 0, 0, tiled=True), axis=0)
    y_parts = split(info, 3, *after(x_parts, result))
    feed_sum = after(feed_sum, y_parts)
    y_parts = spread(y_parts, "y")
    input_other = swap(input_sent, "xl").astype(f32)
    first = xl == 0
    input_grad = jnp.stack([jnp.where(first, input_keep, input_other), jnp.where(first, input_other, input_keep)])

    wide_rate = matrix_rate * MODEL_WIDTH ** (-0.5)
    gate_up_down = adam(
        [feed_sum],
        [gate_weight, gate_first, gate_second, up_weight, up_first, up_second]
        + [down_weight.T, down_first.T, down_second.T],
        (wide_rate, wide_rate, matrix_rate * FF ** (-0.5)),
    )
    attn_new = adam(
        y_parts,
        [query_weight, query_first, query_second, key_weight, key_first, key_second]
        + [value_weight, value_first, value_second, out_weight.T, out_first.T, out_second.T],
        (wide_rate, wide_rate, wide_rate, matrix_rate * WO_FAN ** (-0.5)),
    )
    gains_new = adamw(gains, gain_first, gain_second, gain_sum, gain_rate)
    updates = (*attn_new[:9], *[a.T for a in attn_new[9:]], *gate_up_down[:6], *[a.T for a in gate_up_down[6:]])
    return (result, input_grad, *updates, *gains_new)


def solution(mesh):
    split = Mesh(mesh.devices.reshape(2, 4, 2, 2, 4), ALL)
    rows = P(DP, TENSOR, None)
    wide = (P(DP, TENSOR),) * 3
    tall = (P(TENSOR, DP),) * 3
    flat = (P(DP),) * 3
    weights = wide * 3 + tall + wide * 2 + tall + flat
    return jax.shard_map(
        per_device,
        mesh=split,
        in_specs=(rows, P(DP, None), rows) + weights,
        out_specs=(rows, rows) + weights,
        check_vma=False,
    )
```
